32 devices in a mesh: row: 16 (over z, x, core), col: 2 (over y).
Axes of the slice: x: 2, y: 2, z: 4, core: 2. Of those that a mesh axis runs over, the one named last changes fastest.
Arguments:
- activations: bfloat16 [256, 8192], P('col', 'row'), may hold values from -6 to 6
- cotangent: bfloat16 [256, 14336], P('row', 'col'), may hold values from -0.15625 to 0.15625
- accumulated: bfloat16 [8192, 14336], P('row', 'col'), may hold values from -3 to 3
- band_old: float32 [8192, 8, 512], P('row', 'col'), may hold values from -6 to 6
- diagonal_old: float32 [8192, 512], P(('row', 'col')), may hold values from -6 to 6
Outputs:
- band_new: float32 [8192, 8, 512], P('row', 'col')
- diagonal_new: float32 [8192, 512], P(('row', 'col'))
The draws below stay inside these ranges and needn't reach their ends.
All inputs are finite; a program needn't handle non-finite values.
Results may differ from the reference program's by a relative error of at most 0.0018.
Values may be sent and summed in bfloat16 or wider, within the bound.
No kernel may reach another device: no remote copies, remote signals or barrier semaphores. Data moves between devices by JAX's collectives and lax.ppermute only.
A program may use at most 128 MiB of HBM per device.

```python
import jax
import jax.numpy as jnp
from jax import lax

D = 8192
FF = 14336
TOKENS = 256
BLOCK = 512
BAND = 8
N_ROW = 16


def shard_levels(key, dims, shards, smallest, largest):
    gain = 1.0
    for position, parts in shards:
        draws = jax.random.uniform(jax.random.fold_in(jax.random.fold_in(key, 6), position), (parts,), jnp.float32, smallest / len(shards), largest / len(shards))
        gain = gain * jnp.repeat(jnp.exp(draws), dims[position] // parts).reshape((-1,) + (1,) * (len(dims) - 1 - position))
    return gain


def gaussian(key, dims, width, most, shards=(), kind=jnp.bfloat16):
    loudness = shard_levels(key, dims, shards, -0.22, 0.18) if shards else 1.0
    values = jax.random.normal(key, dims, jnp.float32) * width * loudness
    return jnp.minimum(jnp.maximum(values, -most), most).astype(kind)


def setup_inputs(seed: int = 0) -> dict:
    splits = jax.random.split(jax.random.key(seed), 6)
    activations = gaussian(splits[0], (TOKENS, D), 1.0, 6.0, ((0, 2), (1, 16)))
    cotangent = gaussian(splits[1], (TOKENS, FF), (6 * TOKENS) ** -0.5, 0.15625, ((0, 16), (1, 2)))
    accumulated = gaussian(splits[2], (D, FF), 0.5, 3.0, ((0, 16), (1, 2)))
    band_old = gaussian(splits[3], (D, BAND, BLOCK), 1.0, 6.0, ((0, 16), (1, 2)), jnp.float32)
    diagonal_old = gaussian(splits[4], (D, BLOCK), 1.0, 6.0, ((0, 32),), jnp.float32)
    return {"activations": activations, "cotangent": cotangent, "accumulated": accumulated, "band_old": band_old, "diagonal_old": diagonal_old}


decay_rate = 0.95


def reference(activations, cotangent, accumulated, band_old, diagonal_old):
    product = jnp.dot(activations.T, cotangent, preferred_element_type=jnp.float32)
    gradient = (product + accumulated.astype(jnp.float32)).astype(jnp.bfloat16)
    blocks = gradient.astype(jnp.float32).reshape(N_ROW, D // N_ROW, FF)
    self_gram = jnp.einsum("rak,rbk->rab", blocks, blocks, precision=lax.Precision.HIGHEST)
    band_list = []
    for offset in range(1, N_ROW // 2 + 1):
        shifted = jnp.roll(blocks, offset, axis=0)
        band_list.append(jnp.einsum("rak,rbk->rab", blocks, shifted, precision=lax.Precision.HIGHEST))
    stacked = jnp.stack(band_list, axis=2).reshape(D, N_ROW // 2, D // N_ROW)
    band_new = decay_rate * band_old + (1.0 - decay_rate) * stacked
    diagonal_new = decay_rate * diagonal_old + (1.0 - decay_rate) * self_gram.reshape(D, D // N_ROW)
    return (band_new, diagonal_new)
```

```python
import jax
import jax.numpy as jnp
from jax import lax
from jax.sharding import PartitionSpec as P

decay_rate = 0.95
GROUP = 4


def swap(array, mask):
    count = lax.axis_size("row")
    return lax.ppermute(array, "row", [(i, i ^ mask) for i in range(count)])


def from_behind(array, by):
    count = lax.axis_size("row")
    return lax.ppermute(array, "row", [(i, (i + by) % count) for i in range(count)])


def gradient_tile(columns, cotangent_all, accumulated):
    product = lax.dot_general(
        columns, cotangent_all, (((0,), (0,)), ((), ())), preferred_element_type=jnp.float32
    )
    return (product + accumulated.astype(jnp.float32)).astype(jnp.bfloat16)


def block_product(left, right):
    return lax.dot_general(
        left, right, (((1,), (1,)), ((), ())), preferred_element_type=jnp.float32
    )


def body(activations, cotangent, accumulated, band_old, diagonal_old):
    columns = lax.all_gather(activations, "col", axis=0, tiled=True)
    cotangent_all = lax.all_gather(cotangent, "row", axis=0, tiled=True)
    own = gradient_tile(columns, cotangent_all, accumulated)
    n_row, n_col = lax.axis_size("row"), lax.axis_size("col")
    block = own.shape[0]
    band = n_row // 2
    steps = band // GROUP
    place = lax.axis_index("row") % GROUP
    position = lax.axis_index("col")

    across = swap(own, 2)
    group = [own, swap(own, 1), across, swap(across, 1)]

    blocks = [None] * (steps + 1)
    blocks[steps] = [block_product(own, panel) for panel in group]
    moving = own
    for step in range(1, steps + 1):
        moving = from_behind(moving, GROUP)
        made = [block_product(panel, moving) for panel in group]
        blocks[steps - step] = [made[0]] + [swap(made[u], u) for u in range(1, GROUP)]
    stacked = jnp.stack([piece for row in blocks for piece in row])

    def at(offset):
        t = band + place - offset
        return lax.dynamic_index_in_dim(
            stacked, t - t % GROUP + ((t % GROUP) ^ place), 0, keepdims=False
        )

    share = band // n_col
    summed = lax.psum_scatter(
        jnp.stack([at(s) for s in range(1, band + 1)]), "col", scatter_dimension=0, tiled=True
    )
    diagonal = lax.psum_scatter(
        blocks[steps][0], "col", scatter_dimension=0, tiled=True
    )
    band_new = decay_rate * band_old + (1.0 - decay_rate) * jnp.swapaxes(summed, 0, 1)
    diagonal_new = decay_rate * diagonal_old + (1.0 - decay_rate) * diagonal
    return (band_new, diagonal_new)


def solution(mesh):
    in_specs = (
        P("col", "row"),
        P("row", "col"),
        P("row", "col"),
        P("row", "col", None),
        P(("row", "col"), None),
    )
    out_specs = (P("row", "col", None), P(("row", "col"), None))
    return jax.shard_map(body, mesh=mesh, in_specs=in_specs, out_specs=out_specs, check_vma=False)
```

```python
import jax
import jax.numpy as jnp
from jax import lax
from jax.sharding import PartitionSpec as P

decay_rate = 0.95
GROUP = 4


def swap(array, mask):
    count = lax.axis_size("row")
    return lax.ppermute(array, "row", [(i, i ^ mask) for i in range(count)])


def from_behind(array, by):
    count = lax.axis_size("row")
    return lax.ppermute(array, "row", [(i, (i + by) % count) for i in range(count)])


def gradient_tile(columns, cotangent_all, accumulated):
    product = lax.dot_general(
        columns, cotangent_all, (((0,), (0,)), ((), ())), preferred_element_type=jnp.float32
    )
    return (product + accumulated.astype(jnp.float32)).astype(jnp.bfloat16)


def block_product(left, right):
    return lax.dot_general(
        left, right, (((1,), (1,)), ((), ())), preferred_element_type=jnp.float32
    )


def ring_body(activations, cotangent, accumulated, band_old, diagonal_old):
    columns = lax.all_gather(activations, "col", axis=0, tiled=True)
    cotangent_all = lax.all_gather(cotangent, "row", axis=0, tiled=True)
    own = gradient_tile(columns, cotangent_all, accumulated)
    n_row, n_col = lax.axis_size("row"), lax.axis_size("col")
    block = own.shape[0]
    band = n_row // 2
    steps = band // GROUP
    place = lax.axis_index("row") % GROUP
    position = lax.axis_index("col")

    across = swap(own, 2)
    group = [own, swap(own, 1), across, swap(across, 1)]

    blocks = [None] * (steps + 1)
    blocks[steps] = [block_product(own, panel) for panel in group]
    moving = own
    for step in range(1, steps + 1):
        moving = from_behind(moving, GROUP)
        made = [block_product(panel, moving) for panel in group]
        blocks[steps - step] = [made[0]] + [swap(made[u], u) for u in range(1, GROUP)]
    stacked = jnp.stack([piece for row in blocks for piece in row])

    def at(offset):
        t = band + place - offset
        return lax.dynamic_index_in_dim(
            stacked, t - t % GROUP + ((t % GROUP) ^ place), 0, keepdims=False
        )

    share = band // n_col
    summed = lax.psum_scatter(
        jnp.stack([at(s) for s in range(1, band + 1)]), "col", scatter_dimension=0, tiled=True
    )
    diagonal = lax.psum_scatter(
        blocks[steps][0], "col", scatter_dimension=0, tiled=True
    )
    band_new = decay_rate * band_old + (1.0 - decay_rate) * jnp.swapaxes(summed, 0, 1)
    diagonal_new = decay_rate * diagonal_old + (1.0 - decay_rate) * diagonal
    return (band_new, diagonal_new)


def move(array, pairs):
    return lax.ppermute(
        array,
        "row",
        [(a * GROUP + place, b * GROUP + place) for a, b in pairs for place in range(GROUP)],
    )


def trade(array):
    return lax.ppermute(array, "col", [(0, 1), (1, 0)])


def split_body(activations, cotangent, accumulated, band_old, diagonal_old):
    row, y = lax.axis_index("row"), lax.axis_index("col")
    z, place = row // GROUP, row % GROUP
    outer = (z == 0) | (z == 3)
    upper = z // 2
    block, width = accumulated.shape
    half, cut = width // 2, block // 2
    parts = range(2)

    def side(array, which):
        return lax.dynamic_slice_in_dim(array, which * half, half, 1)

    def part(array, c):
        return array[c * cut : (c + 1) * cut]

    kept, crossing = side(accumulated, upper), side(accumulated, 1 - upper)
    direct = [move(part(crossing, c), [(1, 2), (2, 1)]) for c in parts]
    relay = [move(part(crossing, c), [(0, 1), (3, 2)]) for c in parts]
    across_kept = swap(kept, 2)
    onward = [move(direct[c], [(1, 0), (2, 3)]) for c in parts]
    second = [move(relay[c], [(1, 2), (2, 1)]) for c in parts]
    inner_kept = [move(part(kept, c), [(0, 1), (3, 2)]) for c in parts]
    across_crossing = swap(crossing, 2)
    second_onward = [move(second[c], [(1, 0), (2, 3)]) for c in parts]

    columns = lax.all_gather(activations, "col", axis=0, tiled=True)
    cotangent_all = lax.all_gather(cotangent, "row", axis=0, tiled=True)
    cot_kept, cot_crossing = side(cotangent_all, upper), side(cotangent_all, 1 - upper)
    columns_across = swap(columns, 2)
    columns_inner = swap(columns, GROUP)
    columns_two, columns_three = swap(columns, 2 * GROUP), swap(columns, 3 * GROUP)
    columns_near = jnp.where(outer, columns_two, columns_three)
    columns_far = jnp.where(outer, columns_three, columns_two)

    def group_of(cot, own_raw, across_raw):
        own = gradient_tile(columns, cot, own_raw)
        across = gradient_tile(columns_across, cot, across_raw)
        return [own, swap(own, 1), across, swap(across, 1)]

    group_kept = group_of(cot_kept, kept, across_kept)
    group_crossing = group_of(cot_crossing, crossing, across_crossing)

    def reduced(pieces, c):
        pieces = jnp.stack(pieces)
        keep = c ^ y
        mine = lax.dynamic_slice_in_dim(pieces, keep * cut, cut, 1)
        theirs = lax.dynamic_slice_in_dim(pieces, (1 - keep) * cut, cut, 1)
        return mine + trade(theirs.astype(jnp.bfloat16)).astype(jnp.float32)

    def to_owners(pieces):
        return jnp.stack([pieces[0]] + [swap(pieces[u], u) for u in range(1, GROUP)])

    def tile_part(cols, c):
        return cols[:, c * cut : (c + 1) * cut]

    near, far, inner = [], [], []
    for c in parts:
        panel = gradient_tile(
            tile_part(columns_near, c), cot_kept, jnp.where(outer, onward[c], direct[c])
        )
        near.append(reduced([block_product(left, panel) for left in group_kept], c))
    for c in parts:
        panel = gradient_tile(tile_part(columns_inner, c), cot_kept, inner_kept[c])
        panel_crossing = gradient_tile(tile_part(columns_inner, c), cot_crossing, relay[c])
        inner.append(
            reduced(
                [
                    block_product(left, panel) + block_product(left_crossing, panel_crossing)
                    for left, left_crossing in zip(group_kept, group_crossing)
                ],
                c,
            )
        )
    own_products = [
        block_product(group_kept[0], right) + block_product(group_crossing[0], right_crossing)
        for right, right_crossing in zip(group_kept, group_crossing)
    ]
    for c in parts:
        panel = gradient_tile(
            tile_part(columns_far, c), cot_kept, jnp.where(outer, second_onward[c], second[c])
        )
        far.append(reduced([block_product(left, panel) for left in group_kept], c))

    one_behind, two_behind = [], []
    here = [[to_owners(kind[c]) for c in parts] for kind in (near, inner, far)]
    narrow = [[kind[c].astype(jnp.bfloat16) for c in parts] for kind in (near, inner, far)]
    for c in parts:
        mine = jnp.where(z == 0, here[2][c], jnp.where(z == 2, here[0][c], here[1][c]))
        one_behind.append(jnp.where(z == 3, 0.0, mine))
        two_behind.append(jnp.where(outer, here[0][c], here[2][c]))
    quarters = []
    for h in parts:
        one = [
            move(narrow[0][h], [(1, 2)]),
            move(narrow[1][h], [(2, 3)]),
            move(narrow[2][h], [(3, 0)]),
        ]
        two = [move(narrow[0][h], [(0, 2), (3, 1)]), move(narrow[2][h], [(2, 0), (1, 3)])]
        pieces = []
        for mine, arrived in ((two_behind, two), (one_behind, one)):
            total = sum(a.astype(jnp.float32) for a in arrived)
            pieces.append(
                jnp.where(y == 0, mine[h], mine[1 - h]) + jnp.swapaxes(total, 1, 2)
            )
        quarters.append(jnp.concatenate(pieces))
    quarters = jnp.stack(quarters, axis=1)

    band = 2 * GROUP

    def where_is(offset):
        t = band + place - offset
        u = (t % GROUP) ^ place
        return t, u

    def quarters_of(offset):
        t, u = where_is(offset)
        return lax.dynamic_index_in_dim(
            quarters, jnp.minimum(t // GROUP, 1) * GROUP + u, 0, keepdims=False
        )

    share = band // 2
    theirs = jnp.stack([quarters_of(s + (1 - y) * share) for s in range(1, share + 1)])
    arrived = trade(theirs)
    own_rest = jnp.stack(own_products[1:])
    own_sum = own_rest + trade(own_rest.astype(jnp.bfloat16)).astype(jnp.float32)
    blocks = []
    for s in range(1, share + 1):
        offset = s + y * share
        mine, other = quarters_of(offset), arrived[s - 1]
        even, odd = jnp.where(y == 0, mine, other), jnp.where(y == 0, other, mine)
        whole = jnp.concatenate(
            [
                jnp.concatenate([even[0], odd[0]], axis=1),
                jnp.concatenate([odd[1], even[1]], axis=1),
            ]
        )
        t, u = where_is(offset)
        local = lax.dynamic_index_in_dim(own_sum, jnp.maximum(u - 1, 0), 0, keepdims=False)
        blocks.append(jnp.where(t >= band, local, whole))
    band_new = decay_rate * band_old + (1.0 - decay_rate) * jnp.stack(blocks, axis=1)

    own_own = own_products[0]
    diagonal = lax.dynamic_slice_in_dim(own_own, y * cut, cut, 0) + trade(
        lax.dynamic_slice_in_dim(own_own, (1 - y) * cut, cut, 0)
    )
    diagonal_new = decay_rate * diagonal_old + (1.0 - decay_rate) * diagonal
    return (band_new, diagonal_new)


def solution(mesh):
    line = mesh.shape["row"] == 4 * GROUP and mesh.shape["col"] == 2
    body = split_body if line else ring_body
    in_specs = (
        P("col", "row"),
        P("row", "col"),
        P("row", "col"),
        P("row", "col", None),
        P(("row", "col"), None),
    )
    out_specs = (P("row", "col", None), P(("row", "col"), None))
    return jax.shard_map(body, mesh=mesh, in_specs=in_specs, out_specs=out_specs, check_vma=False)
```

```python
import jax
import jax.numpy as jnp
from jax import lax
from jax.experimental import pallas as pl
from jax.experimental.pallas import tpu as pltpu
from jax.sharding import PartitionSpec as P

decay_rate = 0.95
GROUP = 4
CHUNKS = 2


def swap(array, mask):
    count = lax.axis_size("row")
    return lax.ppermute(array, "row", [(i, i ^ mask) for i in range(count)])


def from_behind(array, by):
    count = lax.axis_size("row")
    return lax.ppermute(array, "row", [(i, (i + by) % count) for i in range(count)])


def trade(array):
    return lax.ppermute(array, "col", [(0, 1), (1, 0)])


def gradient_tile(columns, cotangent_all, accumulated):
    product = lax.dot_general(
        columns, cotangent_all, (((1,), (0,)), ((), ())), preferred_element_type=jnp.float32
    )
    return (product + accumulated.astype(jnp.float32)).astype(jnp.bfloat16)


def block_product(left, right):
    return lax.dot_general(
        left, right, (((1,), (1,)), ((), ())), preferred_element_type=jnp.float32
    )


def products_kernel(*refs):
    *lefts, raw, columns, cotangent, out = refs
    panel = gradient_tile(columns[...], cotangent[...], raw[...])
    parts = [block_product(left[...], panel) for left in lefts]

    @pl.when(pl.program_id(0) == 0)
    def _():
        for u, part in enumerate(parts):
            out[u] = part

    @pl.when(pl.program_id(0) > 0)
    def _():
        for u, part in enumerate(parts):
            out[u] += part


def panel_products(group, raw, columns, cotangent_all):
    block, width = group[0].shape
    rows, tokens = columns.shape
    depth = max(d for d in range(128, 1025, 128) if width % d == 0)
    return pl.pallas_call(
        products_kernel,
        grid=(width // depth,),
        in_specs=[pl.BlockSpec((block, depth), lambda k: (0, k))] * len(group)
        + [
            pl.BlockSpec((rows, depth), lambda k: (0, k)),
            pl.BlockSpec((rows, tokens), lambda k: (0, 0)),
            pl.BlockSpec((tokens, depth), lambda k: (0, k)),
        ],
        out_specs=pl.BlockSpec((len(group), block, rows), lambda k: (0, 0, 0)),
        out_shape=jax.ShapeDtypeStruct((len(group), block, rows), jnp.float32),
        compiler_params=pltpu.CompilerParams(
            dimension_semantics=("arbitrary",), vmem_limit_bytes=48 * 2**20
        ),
        cost_estimate=pl.CostEstimate(
            flops=2 * rows * width * (len(group) * block + tokens),
            bytes_accessed=2 * width * (len(group) * block + rows + tokens)
            + 4 * len(group) * block * rows,
            transcendentals=0,
        ),
    )(*group, raw, columns, cotangent_all)


def body(activations, cotangent, accumulated, band_old, diagonal_old):
    n_row, n_col = lax.axis_size("row"), lax.axis_size("col")
    block, width = accumulated.shape
    band = n_row // 2
    steps = band // GROUP
    place = lax.axis_index("row") % GROUP
    y = lax.axis_index("col")

    columns = lax.all_gather(activations, "col", axis=0, tiled=True)
    parcel = jnp.concatenate([accumulated, columns.T], axis=1)
    moving = from_behind(parcel, GROUP)
    across_parcel = swap(parcel, 2)
    cotangent_all = lax.all_gather(cotangent, "row", axis=0, tiled=True)

    def gradient_of(parcel):
        return gradient_tile(parcel[:, width:], cotangent_all, parcel[:, :width])

    def products(parcel):
        return panel_products(group, parcel[:, :width], parcel[:, width:], cotangent_all)

    def to_owners(made):
        return jnp.stack([made[0]] + [swap(made[u], u) for u in range(1, GROUP)])

    own = gradient_of(parcel)
    across = gradient_of(across_parcel)
    group = [own, swap(own, 1), across, swap(across, 1)]

    sums = [None] * (steps + 1)
    own_products = [block_product(own, panel) for panel in group]
    for step in range(1, steps):
        arrived = moving
        moving = from_behind(arrived, GROUP) if step < steps - 1 else [
            from_behind(piece, GROUP) for piece in jnp.split(arrived, CHUNKS)
        ]
        made = products(arrived)
        if step == steps - 1:
            moving[0], made, own_products = lax.optimization_barrier(
                (moving[0], made, own_products)
            )
        sums[steps - step] = to_owners(made)
    sums[steps] = jnp.stack(own_products)

    if n_col == 2:
        sums[steps] += trade(sums[steps].astype(jnp.bfloat16)).astype(jnp.float32)
        for step in range(1, steps):
            narrow = sums[steps - step].astype(jnp.bfloat16)
            sums[steps - step] += trade(narrow).astype(jnp.float32)
    last = []
    for piece in moving:
        part = to_owners(products(piece))
        if n_col == 2:
            part += trade(part.astype(jnp.bfloat16)).astype(jnp.float32)
        last.append(part)
    sums[0] = jnp.concatenate(last, axis=2)
    stacked = jnp.concatenate(sums)

    def at(offset):
        t = band + place - offset
        return lax.dynamic_index_in_dim(
            stacked, t - t % GROUP + ((t % GROUP) ^ place), 0, keepdims=False
        )

    share = band // n_col
    if n_col == 2:
        band_sum = jnp.stack([at(s + y * share) for s in range(1, share + 1)], axis=1)
        diagonal = lax.dynamic_slice_in_dim(sums[steps][0], y * (block // 2), block // 2, 0)
    else:
        band_sum = jnp.swapaxes(
            lax.psum_scatter(
                jnp.stack([at(s) for s in range(1, band + 1)]),
                "col",
                scatter_dimension=0,
                tiled=True,
            ),
            0,
            1,
        )
        diagonal = lax.psum_scatter(own_products[0], "col", scatter_dimension=0, tiled=True)
    band_new = decay_rate * band_old + (1.0 - decay_rate) * band_sum
    diagonal_new = decay_rate * diagonal_old + (1.0 - decay_rate) * diagonal
    return (band_new, diagonal_new)


def solution(mesh):
    in_specs = (
        P("col", "row"),
        P("row", "col"),
        P("row", "col"),
        P("row", "col", None),
        P(("row", "col"), None),
    )
    out_specs = (P("row", "col", None), P(("row", "col"), None))
    return jax.shard_map(body, mesh=mesh, in_specs=in_specs, out_specs=out_specs, check_vma=False)
```

```python
import jax
import jax.numpy as jnp
from jax import lax
from jax.experimental import pallas as pl
from jax.experimental.pallas import tpu as pltpu
from jax.sharding import PartitionSpec as P

decay_rate = 0.95
GROUP = 4


def swap(array, mask):
    count = lax.axis_size("row")
    return lax.ppermute(array, "row", [(i, i ^ mask) for i in range(count)])


def from_behind(array, by):
    count = lax.axis_size("row")
    return lax.ppermute(array, "row", [(i, (i + by) % count) for i in range(count)])


def trade(array):
    return lax.ppermute(array, "col", [(0, 1), (1, 0)])


def gradient_tile(columns, cotangent_all, accumulated):
    product = lax.dot_general(
        columns, cotangent_all, (((1,), (0,)), ((), ())), preferred_element_type=jnp.float32
    )
    return (product + accumulated.astype(jnp.float32)).astype(jnp.bfloat16)


def block_product(left, right):
    return lax.dot_general(
        left, right, (((1,), (1,)), ((), ())), preferred_element_type=jnp.float32
    )


def products_kernel(*refs):
    *lefts, raw, columns, cotangent, out = refs
    panel = gradient_tile(columns[...], cotangent[...], raw[...])
    parts = [block_product(left[...], panel) for left in lefts]

    @pl.when(pl.program_id(0) == 0)
    def _():
        for u, part in enumerate(parts):
            out[u] = part

    @pl.when(pl.program_id(0) > 0)
    def _():
        for u, part in enumerate(parts):
            out[u] += part


def panel_products(group, raw, columns, cotangent_all):
    block, width = group[0].shape
    rows, tokens = columns.shape
    depth = max(d for d in range(128, 1025, 128) if width % d == 0)
    return pl.pallas_call(
        products_kernel,
        grid=(width // depth,),
        in_specs=[pl.BlockSpec((block, depth), lambda k: (0, k))] * len(group)
        + [
            pl.BlockSpec((rows, depth), lambda k: (0, k)),
            pl.BlockSpec((rows, tokens), lambda k: (0, 0)),
            pl.BlockSpec((tokens, depth), lambda k: (0, k)),
        ],
        out_specs=pl.BlockSpec((len(group), block, rows), lambda k: (0, 0, 0)),
        out_shape=jax.ShapeDtypeStruct((len(group), block, rows), jnp.float32),
        compiler_params=pltpu.CompilerParams(
            dimension_semantics=("arbitrary",), vmem_limit_bytes=48 * 2**20
        ),
        cost_estimate=pl.CostEstimate(
            flops=2 * rows * width * (len(group) * block + tokens),
            bytes_accessed=2 * width * (len(group) * block + rows + tokens)
            + 4 * len(group) * block * rows,
            transcendentals=0,
        ),
    )(*group, raw, columns, cotangent_all)


def body(activations, cotangent, accumulated, band_old, diagonal_old):
    n_row, n_col = lax.axis_size("row"), lax.axis_size("col")
    block, width = accumulated.shape
    band = n_row // 2
    steps = band // GROUP
    place = lax.axis_index("row") % GROUP
    y = lax.axis_index("col")

    columns = lax.all_gather(activations, "col", axis=0, tiled=True)
    parcel = jnp.concatenate([accumulated, columns.T], axis=1)
    moving = from_behind(parcel, GROUP)
    across_parcel = swap(parcel, 2)
    cotangent_all = lax.all_gather(cotangent, "row", axis=0, tiled=True)

    def gradient_of(parcel):
        return gradient_tile(parcel[:, width:], cotangent_all, parcel[:, :width])

    def products(parcel):
        return panel_products(group, parcel[:, :width], parcel[:, width:], cotangent_all)

    def to_owners(made):
        return jnp.stack([made[0]] + [swap(made[u], u) for u in range(1, GROUP)])

    own = gradient_of(parcel)
    across = gradient_of(across_parcel)
    group = [own, swap(own, 1), across, swap(across, 1)]

    sums = [None] * (steps + 1)
    own_products = [block_product(own, panel) for panel in group]
    for step in range(1, steps):
        arrived = moving
        moving = from_behind(arrived, GROUP) if step < steps - 1 else [
            from_behind(piece, GROUP)
            for piece in jnp.split(arrived, [block // 2, 3 * block // 4])
        ]
        made = products(arrived)
        if step == steps - 1:
            moving[0], made, own_products = lax.optimization_barrier(
                (moving[0], made, own_products)
            )
        sums[steps - step] = to_owners(made)
    sums[steps] = jnp.stack(own_products)

    if n_col == 2:
        sums[steps] += trade(sums[steps].astype(jnp.bfloat16)).astype(jnp.float32)
        for step in range(1, steps):
            narrow = sums[steps - step].astype(jnp.bfloat16)
            sums[steps - step] += trade(narrow).astype(jnp.float32)
    last = []
    for piece in moving:
        if last:
            piece, sums[1:], last = lax.optimization_barrier((piece, sums[1:], last))
        part = to_owners(products(piece))
        if n_col == 2:
            part += trade(part.astype(jnp.bfloat16)).astype(jnp.float32)
        last.append(part)
    sums[0] = jnp.concatenate(last, axis=2)
    stacked = jnp.concatenate(sums)

    def at(offset):
        t = band + place - offset
        return lax.dynamic_index_in_dim(
            stacked, t - t % GROUP + ((t % GROUP) ^ place), 0, keepdims=False
        )

    share = band // n_col
    if n_col == 2:
        band_sum = jnp.stack([at(s + y * share) for s in range(1, share + 1)], axis=1)
        diagonal = lax.dynamic_slice_in_dim(sums[steps][0], y * (block // 2), block // 2, 0)
    else:
        band_sum = jnp.swapaxes(
            lax.psum_scatter(
                jnp.stack([at(s) for s in range(1, band + 1)]),
                "col",
                scatter_dimension=0,
                tiled=True,
            ),
            0,
            1,
        )
        diagonal = lax.psum_scatter(own_products[0], "col", scatter_dimension=0, tiled=True)
    band_new = decay_rate * band_old + (1.0 - decay_rate) * band_sum
    diagonal_new = decay_rate * diagonal_old + (1.0 - decay_rate) * diagonal
    return (band_new, diagonal_new)


def solution(mesh):
    in_specs = (
        P("col", "row"),
        P("row", "col"),
        P("row", "col"),
        P("row", "col", None),
        P(("row", "col"), None),
    )
    out_specs = (P("row", "col", None), P(("row", "col"), None))
    return jax.shard_map(body, mesh=mesh, in_specs=in_specs, out_specs=out_specs, check_vma=False)
```

```python
import jax
import jax.numpy as jnp
from jax import lax
from jax.experimental import pallas as pl
from jax.experimental.pallas import tpu as pltpu
from jax.sharding import PartitionSpec as P

decay_rate = 0.95
GROUP = 4


def swap(array, mask):
    count = lax.axis_size("row")
    return lax.ppermute(array, "row", [(i, i ^ mask) for i in range(count)])


def from_behind(array, by):
    count = lax.axis_size("row")
    return lax.ppermute(array, "row", [(i, (i + by) % count) for i in range(count)])


def trade(array):
    return lax.ppermute(array, "col", [(0, 1), (1, 0)])


def gradient_tile(columns, cotangent_all, accumulated):
    product = lax.dot_general(
        columns, cotangent_all, (((1,), (0,)), ((), ())), preferred_element_type=jnp.float32
    )
    return (product + accumulated.astype(jnp.float32)).astype(jnp.bfloat16)


def block_product(left, right):
    return lax.dot_general(
        left, right, (((1,), (1,)), ((), ())), preferred_element_type=jnp.float32
    )


def products_kernel(*refs):
    *lefts, raw, columns, cotangent, out = refs
    panel = gradient_tile(columns[...], cotangent[...], raw[...])
    parts = [block_product(left[...], panel) for left in lefts]

    @pl.when(pl.program_id(0) == 0)
    def _():
        for u, part in enumerate(parts):
            out[u] = part

    @pl.when(pl.program_id(0) > 0)
    def _():
        for u, part in enumerate(parts):
            out[u] += part


def panel_products(group, raw, columns, cotangent_all):
    block, width = group[0].shape
    rows, tokens = columns.shape
    depth = max(d for d in range(128, 1025, 128) if width % d == 0)
    return pl.pallas_call(
        products_kernel,
        grid=(width // depth,),
        in_specs=[pl.BlockSpec((block, depth), lambda k: (0, k))] * len(group)
        + [
            pl.BlockSpec((rows, depth), lambda k: (0, k)),
            pl.BlockSpec((rows, tokens), lambda k: (0, 0)),
            pl.BlockSpec((tokens, depth), lambda k: (0, k)),
        ],
        out_specs=pl.BlockSpec((len(group), block, rows), lambda k: (0, 0, 0)),
        out_shape=jax.ShapeDtypeStruct((len(group), block, rows), jnp.float32),
        compiler_params=pltpu.CompilerParams(
            dimension_semantics=("arbitrary",), vmem_limit_bytes=48 * 2**20
        ),
        cost_estimate=pl.CostEstimate(
            flops=2 * rows * width * (len(group) * block + tokens),
            bytes_accessed=2 * width * (len(group) * block + rows + tokens)
            + 4 * len(group) * block * rows,
            transcendentals=0,
        ),
    )(*group, raw, columns, cotangent_all)


def body(activations, cotangent, accumulated, band_old, diagonal_old):
    n_row, n_col = lax.axis_size("row"), lax.axis_size("col")
    block, width = accumulated.shape
    band = n_row // 2
    steps = band // GROUP
    place = lax.axis_index("row") % GROUP
    y = lax.axis_index("col")

    phase = lax.optimization_barrier

    columns = lax.all_gather(activations, "col", axis=0, tiled=True)
    parcel = jnp.concatenate([accumulated, columns.T], axis=1)
    moving = from_behind(parcel, GROUP)
    across_parcel = swap(parcel, 2)
    cotangent_all = lax.all_gather(cotangent, "row", axis=0, tiled=True)

    def gradient_of(parcel):
        return gradient_tile(parcel[:, width:], cotangent_all, parcel[:, :width])

    def products(parcel):
        return panel_products(group, parcel[:, :width], parcel[:, width:], cotangent_all)

    def to_owners(made):
        return [made[0]] + [swap(made[u], u) for u in range(1, GROUP)]

    def over_columns(sums):
        if n_col != 2:
            return jnp.stack(sums)
        sums = jnp.stack(sums)
        return sums + trade(sums.astype(jnp.bfloat16)).astype(jnp.float32)

    own = gradient_of(parcel)
    beside = swap(own, 1)
    own_products = [block_product(own, panel) for panel in (own, beside)]
    moving, across_parcel, beside, own_products = phase(
        (moving, across_parcel, beside, own_products)
    )

    sums = [None] * (steps + 1)
    made, handed = None, None
    for step in range(1, steps):
        arrived = moving
        quarters = jnp.split(arrived, 4)
        first = from_behind(quarters[0], GROUP)
        if step == 1:
            across = gradient_of(across_parcel)
            group = [own, beside, across, swap(across, 1)]
        else:
            handed = to_owners(made)
        first, group, handed = phase((first, group, handed))
        if step > 1:
            sums[steps - step + 1] = over_columns(handed)
        second = from_behind(quarters[1], GROUP)
        made = products(arrived)
        first, second, made, sums = phase((first, second, made, sums))
        if step < steps - 1:
            rest = [from_behind(piece, GROUP) for piece in quarters[2:]]
            moving = jnp.concatenate([first, second, *rest])

    half = jnp.concatenate([first, second])
    third = from_behind(quarters[2], GROUP)
    handed = to_owners(made)
    made = products(half)
    own_products += [block_product(own, panel) for panel in group[2:]]
    third, handed, made, own_products = phase((third, handed, made, own_products))

    fourth = from_behind(quarters[3], GROUP)
    sums[1] = over_columns(handed)
    handed = to_owners(made)
    made = products(third)
    fourth, sums[1], handed, made = phase((fourth, sums[1], handed, made))

    sums[steps] = over_columns(own_products)
    last = [over_columns(handed)]
    handed = to_owners(made)
    made = products(fourth)
    last, handed, made = phase((last, handed, made))

    last.append(over_columns(handed))
    handed = to_owners(made)
    last, handed = phase((last, handed))
    last.append(over_columns(handed))
    sums[0] = jnp.concatenate(last, axis=2)
    stacked = jnp.concatenate(sums)

    def at(offset):
        t = band + place - offset
        return lax.dynamic_index_in_dim(
            stacked, t - t % GROUP + ((t % GROUP) ^ place), 0, keepdims=False
        )

    share = band // n_col
    if n_col == 2:
        band_sum = jnp.stack([at(s + y * share) for s in range(1, share + 1)], axis=1)
        diagonal = lax.dynamic_slice_in_dim(sums[steps][0], y * (block // 2), block // 2, 0)
    else:
        band_sum = jnp.swapaxes(
            lax.psum_scatter(
                jnp.stack([at(s) for s in range(1, band + 1)]),
                "col",
                scatter_dimension=0,
                tiled=True,
            ),
            0,
            1,
        )
        diagonal = lax.psum_scatter(own_products[0], "col", scatter_dimension=0, tiled=True)
    band_new = decay_rate * band_old + (1.0 - decay_rate) * band_sum
    diagonal_new = decay_rate * diagonal_old + (1.0 - decay_rate) * diagonal
    return (band_new, diagonal_new)


def solution(mesh):
    in_specs = (
        P("col", "row"),
        P("row", "col"),
        P("row", "col"),
        P("row", "col", None),
        P(("row", "col"), None),
    )
    out_specs = (P("row", "col", None), P(("row", "col"), None))
    return jax.shard_map(body, mesh=mesh, in_specs=in_specs, out_specs=out_specs, check_vma=False)
```

```python
import jax
import jax.numpy as jnp
from jax import lax
from jax.experimental import pallas as pl
from jax.experimental.pallas import tpu as pltpu
from jax.sharding import PartitionSpec as P

decay_rate = 0.95
GROUP = 4


def swap(array, mask):
    count = lax.axis_size("row")
    return lax.ppermute(array, "row", [(i, i ^ mask) for i in range(count)])


def from_behind(array, by):
    count = lax.axis_size("row")
    return lax.ppermute(array, "row", [(i, (i + by) % count) for i in range(count)])


def trade(array):
    return lax.ppermute(array, "col", [(0, 1), (1, 0)])


def gradient_tile(columns, cotangent_all, accumulated):
    product = lax.dot_general(
        columns, cotangent_all, (((1,), (0,)), ((), ())), preferred_element_type=jnp.float32
    )
    return (product + accumulated.astype(jnp.float32)).astype(jnp.bfloat16)


def block_product(left, right):
    return lax.dot_general(
        left, right, (((1,), (1,)), ((), ())), preferred_element_type=jnp.float32
    )


def products_kernel(*refs):
    *lefts, raw, columns, cotangent, out = refs
    panel = gradient_tile(columns[...], cotangent[...], raw[...])
    parts = [block_product(left[...], panel) for left in lefts]

    @pl.when(pl.program_id(0) == 0)
    def _():
        for u, part in enumerate(parts):
            out[u] = part

    @pl.when(pl.program_id(0) > 0)
    def _():
        for u, part in enumerate(parts):
            out[u] += part


def panel_products(group, raw, columns, cotangent_all):
    block, width = group[0].shape
    rows, tokens = columns.shape
    depth = max(d for d in range(128, 1025, 128) if width % d == 0)
    return pl.pallas_call(
        products_kernel,
        grid=(width // depth,),
        in_specs=[pl.BlockSpec((block, depth), lambda k: (0, k))] * len(group)
        + [
            pl.BlockSpec((rows, depth), lambda k: (0, k)),
            pl.BlockSpec((rows, tokens), lambda k: (0, 0)),
            pl.BlockSpec((tokens, depth), lambda k: (0, k)),
        ],
        out_specs=pl.BlockSpec((len(group), block, rows), lambda k: (0, 0, 0)),
        out_shape=jax.ShapeDtypeStruct((len(group), block, rows), jnp.float32),
        compiler_params=pltpu.CompilerParams(
            dimension_semantics=("arbitrary",), vmem_limit_bytes=48 * 2**20
        ),
        cost_estimate=pl.CostEstimate(
            flops=2 * rows * width * (len(group) * block + tokens),
            bytes_accessed=2 * width * (len(group) * block + rows + tokens)
            + 4 * len(group) * block * rows,
            transcendentals=0,
        ),
    )(*group, raw, columns, cotangent_all)


def body(activations, cotangent, accumulated, band_old, diagonal_old):
    n_row, n_col = lax.axis_size("row"), lax.axis_size("col")
    block, width = accumulated.shape
    band = n_row // 2
    steps = band // GROUP
    place = lax.axis_index("row") % GROUP
    y = lax.axis_index("col")

    phase = lax.optimization_barrier

    columns = lax.all_gather(activations, "col", axis=0, tiled=True)
    parcel = jnp.concatenate([accumulated, columns.T], axis=1)
    moving = from_behind(parcel, GROUP)
    across_parcel = swap(parcel, 2)
    cotangent_all = lax.all_gather(cotangent, "row", axis=0, tiled=True)

    def gradient_of(parcel):
        return gradient_tile(parcel[:, width:], cotangent_all, parcel[:, :width])

    def products(parcel):
        return panel_products(group, parcel[:, :width], parcel[:, width:], cotangent_all)

    def to_owners(made):
        return [made[0]] + [swap(made[u], u) for u in range(1, GROUP)]

    def over_columns(sums):
        if n_col != 2:
            return jnp.stack(sums)
        sums = jnp.stack(sums)
        return sums + trade(sums.astype(jnp.bfloat16)).astype(jnp.float32)

    moving, across_parcel = phase((moving, across_parcel))
    own = gradient_of(parcel)
    beside = swap(own, 1)

    sums = [None] * (steps + 1)
    made, handed = None, None
    for step in range(1, steps):
        arrived = moving
        quarters = jnp.split(arrived, 4)
        first = from_behind(quarters[0], GROUP)
        if step == 1:
            across = gradient_of(across_parcel)
            group = [own, beside, across, swap(across, 1)]
            own_products = [block_product(own, panel) for panel in (own, beside)]
        else:
            handed = to_owners(made)
        first, group, handed, own_products = phase((first, group, handed, own_products))
        if step > 1:
            sums[steps - step + 1] = over_columns(handed)
        second = from_behind(quarters[1], GROUP)
        made = products(arrived)
        if step == 1:
            own_products += [block_product(own, panel) for panel in group[2:]]
        first, second, made, sums, own_products = phase(
            (first, second, made, sums, own_products)
        )
        if step < steps - 1:
            rest = [from_behind(piece, GROUP) for piece in quarters[2:]]
            moving = jnp.concatenate([first, second, *rest])

    half = jnp.concatenate([first, second])
    third = from_behind(quarters[2], GROUP)
    sums[steps] = over_columns(own_products)
    handed = to_owners(made)
    made = products(half)
    third, handed, made, sums[steps] = phase((third, handed, made, sums[steps]))

    fourth = from_behind(quarters[3], GROUP)
    sums[1] = over_columns(handed)
    handed = to_owners(made)
    made = products(third)
    fourth, sums[1], handed, made = phase((fourth, sums[1], handed, made))

    last = [over_columns(handed)]
    handed = to_owners(made)
    made = products(fourth)
    last, handed, made = phase((last, handed, made))

    last.append(over_columns(handed))
    handed = to_owners(made)
    last, handed = phase((last, handed))
    last.append(over_columns(handed))
    sums[0] = jnp.concatenate(last, axis=2)
    stacked = jnp.concatenate(sums)

    def at(offset):
        t = band + place - offset
        return lax.dynamic_index_in_dim(
            stacked, t - t % GROUP + ((t % GROUP) ^ place), 0, keepdims=False
        )

    share = band // n_col
    if n_col == 2:
        band_sum = jnp.stack([at(s + y * share) for s in range(1, share + 1)], axis=1)
        diagonal = lax.dynamic_slice_in_dim(sums[steps][0], y * (block // 2), block // 2, 0)
    else:
        band_sum = jnp.swapaxes(
            lax.psum_scatter(
                jnp.stack([at(s) for s in range(1, band + 1)]),
                "col",
                scatter_dimension=0,
                tiled=True,
            ),
            0,
            1,
        )
        diagonal = lax.psum_scatter(own_products[0], "col", scatter_dimension=0, tiled=True)
    band_new = decay_rate * band_old + (1.0 - decay_rate) * band_sum
    diagonal_new = decay_rate * diagonal_old + (1.0 - decay_rate) * diagonal
    return (band_new, diagonal_new)


def solution(mesh):
    in_specs = (
        P("col", "row"),
        P("row", "col"),
        P("row", "col"),
        P("row", "col", None),
        P(("row", "col"), None),
    )
    out_specs = (P("row", "col", None), P(("row", "col"), None))
    return jax.shard_map(body, mesh=mesh, in_specs=in_specs, out_specs=out_specs, check_vma=False)
```

```python
import jax
import jax.numpy as jnp
from jax import lax
from jax.experimental import pallas as pl
from jax.experimental.pallas import tpu as pltpu
from jax.sharding import PartitionSpec as P

decay_rate = 0.95
GROUP = 4


def swap(array, mask):
    count = lax.axis_size("row")
    return lax.ppermute(array, "row", [(i, i ^ mask) for i in range(count)])


def from_behind(array, by):
    count = lax.axis_size("row")
    return lax.ppermute(array, "row", [(i, (i + by) % count) for i in range(count)])


def trade(array):
    return lax.ppermute(array, "col", [(0, 1), (1, 0)])


def gradient_tile(columns, cotangent_all, accumulated):
    product = lax.dot_general(
        columns, cotangent_all, (((0,), (0,)), ((), ())), preferred_element_type=jnp.float32
    )
    return (product + accumulated.astype(jnp.float32)).astype(jnp.bfloat16)


def block_product(left, right):
    return lax.dot_general(
        left, right, (((1,), (1,)), ((), ())), preferred_element_type=jnp.float32
    )


def products_kernel(*refs):
    *panels, columns, cotangent, out = refs
    lefts, raws = panels[:GROUP], panels[GROUP:]
    raw = jnp.concatenate([piece[...] for piece in raws])
    panel = gradient_tile(columns[...], cotangent[...], raw)
    parts = [block_product(left[...], panel) for left in lefts]

    @pl.when(pl.program_id(0) == 0)
    def _():
        for u, part in enumerate(parts):
            out[u] = part

    @pl.when(pl.program_id(0) > 0)
    def _():
        for u, part in enumerate(parts):
            out[u] += part


def panel_products(group, raws, columns, cotangent_all):
    block, width = group[0].shape
    tokens, rows = columns.shape
    depth = max(d for d in range(128, 1025, 128) if width % d == 0)
    return pl.pallas_call(
        products_kernel,
        grid=(width // depth,),
        in_specs=[pl.BlockSpec((block, depth), lambda k: (0, k))] * len(group)
        + [pl.BlockSpec((raw.shape[0], depth), lambda k: (0, k)) for raw in raws]
        + [
            pl.BlockSpec((tokens, rows), lambda k: (0, 0)),
            pl.BlockSpec((tokens, depth), lambda k: (0, k)),
        ],
        out_specs=pl.BlockSpec((len(group), block, rows), lambda k: (0, 0, 0)),
        out_shape=jax.ShapeDtypeStruct((len(group), block, rows), jnp.float32),
        compiler_params=pltpu.CompilerParams(
            dimension_semantics=("arbitrary",), vmem_limit_bytes=48 * 2**20
        ),
        cost_estimate=pl.CostEstimate(
            flops=2 * rows * width * (len(group) * block + tokens),
            bytes_accessed=2 * width * (len(group) * block + rows + tokens)
            + 4 * len(group) * block * rows,
            transcendentals=0,
        ),
    )(*group, *raws, columns, cotangent_all)


def body(activations, cotangent, accumulated, band_old, diagonal_old):
    n_row, n_col = lax.axis_size("row"), lax.axis_size("col")
    block, width = accumulated.shape
    band = n_row // 2
    steps = band // GROUP
    place = lax.axis_index("row") % GROUP
    y = lax.axis_index("col")

    phase = lax.optimization_barrier

    quarter = block // 4
    quarters = [
        from_behind(accumulated[q * quarter : (q + 1) * quarter], GROUP) for q in range(4)
    ]
    across_raw = swap(accumulated, 2)
    if n_col == 2:
        other = trade(activations)
        columns = jnp.where(
            y == 0,
            jnp.concatenate([activations, other]),
            jnp.concatenate([other, activations]),
        )
    else:
        columns = lax.all_gather(activations, "col", axis=0, tiled=True)
    across_columns = swap(columns, 2)
    behind = from_behind(columns, GROUP)
    cotangent_all = lax.all_gather(cotangent, "row", axis=0, tiled=True)

    def products(raws, columns):
        return panel_products(group, raws, columns, cotangent_all)

    def to_owners(made):
        return [made[0]] + [swap(made[u], u) for u in range(1, GROUP)]

    def over_columns(sums):
        if n_col != 2:
            return jnp.stack(sums)
        sums = jnp.stack(sums)
        return sums + trade(sums.astype(jnp.bfloat16)).astype(jnp.float32)

    across = gradient_tile(across_columns, cotangent_all, across_raw)
    quarters, behind, across = phase((quarters, behind, across))
    own = gradient_tile(columns, cotangent_all, accumulated)
    beside = swap(own, 1)

    sums = [None] * (steps + 1)
    made, handed = None, None
    for step in range(1, steps):
        arrived, arrived_columns = quarters, behind
        behind = from_behind(arrived_columns, GROUP)
        first = from_behind(arrived[0], GROUP)
        if step == 1:
            group = [own, beside, across, swap(across, 1)]
            own_products = [block_product(own, panel) for panel in (own, beside)]
        else:
            handed = to_owners(made)
        first, group, handed, own_products = phase((first, group, handed, own_products))
        if step > 1:
            sums[steps - step + 1] = over_columns(handed)
        second = from_behind(arrived[1], GROUP)
        made = products(arrived, arrived_columns)
        if step == 1:
            own_products += [block_product(own, panel) for panel in group[2:]]
        first, second, behind, made, sums, own_products = phase(
            (first, second, behind, made, sums, own_products)
        )
        if step < steps - 1:
            rest = [from_behind(piece, GROUP) for piece in arrived[2:]]
            quarters = [first, second, *rest]

    third = from_behind(arrived[2], GROUP)
    sums[steps] = over_columns(own_products)
    handed = to_owners(made)
    made = products([first, second], behind[:, : 2 * quarter])
    third, handed, made, sums[steps] = phase((third, handed, made, sums[steps]))

    fourth = from_behind(arrived[3], GROUP)
    sums[1] = over_columns(handed)
    handed = to_owners(made)
    made = products([third], behind[:, 2 * quarter : 3 * quarter])
    fourth, sums[1], handed, made = phase((fourth, sums[1], handed, made))

    last = [over_columns(handed)]
    handed = to_owners(made)
    made = products([fourth], behind[:, 3 * quarter :])
    last, handed, made = phase((last, handed, made))

    last.append(over_columns(handed))
    handed = to_owners(made)
    last, handed = phase((last, handed))
    last.append(over_columns(handed))
    sums[0] = jnp.concatenate(last, axis=2)
    stacked = jnp.concatenate(sums)

    def at(offset):
        t = band + place - offset
        return lax.dynamic_index_in_dim(
            stacked, t - t % GROUP + ((t % GROUP) ^ place), 0, keepdims=False
        )

    share = band // n_col
    if n_col == 2:
        band_sum = jnp.stack([at(s + y * share) for s in range(1, share + 1)], axis=1)
        diagonal = lax.dynamic_slice_in_dim(sums[steps][0], y * (block // 2), block // 2, 0)
    else:
        band_sum = jnp.swapaxes(
            lax.psum_scatter(
                jnp.stack([at(s) for s in range(1, band + 1)]),
                "col",
                scatter_dimension=0,
                tiled=True,
            ),
            0,
            1,
        )
        diagonal = lax.psum_scatter(own_products[0], "col", scatter_dimension=0, tiled=True)
    band_new = decay_rate * band_old + (1.0 - decay_rate) * band_sum
    diagonal_new = decay_rate * diagonal_old + (1.0 - decay_rate) * diagonal
    return (band_new, diagonal_new)


def solution(mesh):
    in_specs = (
        P("col", "row"),
        P("row", "col"),
        P("row", "col"),
        P("row", "col", None),
        P(("row", "col"), None),
    )
    out_specs = (P("row", "col", None), P(("row", "col"), None))
    return jax.shard_map(body, mesh=mesh, in_specs=in_specs, out_specs=out_specs, check_vma=False)
```

```python
import jax
import jax.numpy as jnp
from jax import lax
from jax.experimental import pallas as pl
from jax.experimental.pallas import tpu as pltpu
from jax.sharding import PartitionSpec as P

decay_rate = 0.95
GROUP = 4


def swap(array, mask):
    count = lax.axis_size("row")
    return lax.ppermute(array, "row", [(i, i ^ mask) for i in range(count)])


def from_behind(array, by):
    count = lax.axis_size("row")
    return lax.ppermute(array, "row", [(i, (i + by) % count) for i in range(count)])


def trade(array):
    return lax.ppermute(array, "col", [(0, 1), (1, 0)])


def gradient_tile(columns, cotangent_all, accumulated):
    product = lax.dot_general(
        columns, cotangent_all, (((0,), (0,)), ((), ())), preferred_element_type=jnp.float32
    )
    return (product + accumulated.astype(jnp.float32)).astype(jnp.bfloat16)


def block_product(left, right):
    return lax.dot_general(
        left, right, (((1,), (1,)), ((), ())), preferred_element_type=jnp.float32
    )


def products_kernel(*refs):
    *panels, columns, cotangent, out = refs
    lefts, raws = panels[:GROUP], panels[GROUP:]
    raw = jnp.concatenate([piece[...] for piece in raws])
    panel = gradient_tile(columns[...], cotangent[...], raw)
    parts = [block_product(left[...], panel) for left in lefts]

    @pl.when(pl.program_id(0) == 0)
    def _():
        for u, part in enumerate(parts):
            out[u] = part

    @pl.when(pl.program_id(0) > 0)
    def _():
        for u, part in enumerate(parts):
            out[u] += part


def panel_products(group, raws, columns, cotangent_all):
    block, width = group[0].shape
    tokens, rows = columns.shape
    depth = max(d for d in range(128, 1025, 128) if width % d == 0)
    return pl.pallas_call(
        products_kernel,
        grid=(width // depth,),
        in_specs=[pl.BlockSpec((block, depth), lambda k: (0, k))] * len(group)
        + [pl.BlockSpec((raw.shape[0], depth), lambda k: (0, k)) for raw in raws]
        + [
            pl.BlockSpec((tokens, rows), lambda k: (0, 0)),
            pl.BlockSpec((tokens, depth), lambda k: (0, k)),
        ],
        out_specs=pl.BlockSpec((len(group), block, rows), lambda k: (0, 0, 0)),
        out_shape=jax.ShapeDtypeStruct((len(group), block, rows), jnp.float32),
        compiler_params=pltpu.CompilerParams(
            dimension_semantics=("arbitrary",), vmem_limit_bytes=48 * 2**20
        ),
        cost_estimate=pl.CostEstimate(
            flops=2 * rows * width * (len(group) * block + tokens),
            bytes_accessed=2 * width * (len(group) * block + rows + tokens)
            + 4 * len(group) * block * rows,
            transcendentals=0,
        ),
    )(*group, *raws, columns, cotangent_all)


def body(activations, cotangent, accumulated, band_old, diagonal_old):
    n_row, n_col = lax.axis_size("row"), lax.axis_size("col")
    block, width = accumulated.shape
    band = n_row // 2
    steps = band // GROUP
    place = lax.axis_index("row") % GROUP
    y = lax.axis_index("col")

    phase = lax.optimization_barrier

    quarter = block // 4
    moving = from_behind(accumulated, GROUP)
    if n_col == 2:
        other = trade(activations)
        columns = jnp.where(
            y == 0,
            jnp.concatenate([activations, other]),
            jnp.concatenate([other, activations]),
        )
    else:
        columns = lax.all_gather(activations, "col", axis=0, tiled=True)
    behind = from_behind(columns, GROUP)
    across_columns, to_cross = phase((swap(columns, 2), accumulated))
    across_raw = swap(to_cross, 2)
    cotangent_all = lax.all_gather(cotangent, "row", axis=0, tiled=True)

    def products(raws, columns):
        return panel_products(group, raws, columns, cotangent_all)

    def to_owners(made):
        return [made[0]] + [swap(made[u], u) for u in range(1, GROUP)]

    def over_columns(sums):
        if n_col != 2:
            return jnp.stack(sums)
        sums = jnp.stack(sums)
        return sums + trade(sums.astype(jnp.bfloat16)).astype(jnp.float32)

    own = gradient_tile(columns, cotangent_all, accumulated)
    beside = swap(own, 1)
    moving, behind, own, beside = phase((moving, behind, own, beside))

    sums = [None] * (steps + 1)
    made = None
    for step in range(1, steps):
        arrived, arrived_columns = moving, behind
        behind = from_behind(arrived_columns, GROUP)
        if step < steps - 1:
            moving = from_behind(arrived, GROUP)
        else:
            quarters = jnp.split(arrived, 4)
            moving = from_behind(jnp.concatenate(quarters[:2]), GROUP)
        if step == 1:
            own_products = [block_product(own, panel) for panel in (own, beside)]
            across = gradient_tile(across_columns, cotangent_all, across_raw)
            group = [own, beside, across, swap(across, 1)]
            own_products += [block_product(own, panel) for panel in group[2:]]
        else:
            sums[steps - step + 1] = over_columns(to_owners(made))
        made = products([arrived], arrived_columns)
        moving, behind, made, sums, own_products = phase(
            (moving, behind, made, sums, own_products)
        )

    third = from_behind(quarters[2], GROUP)
    sums[steps] = over_columns(own_products)
    handed = to_owners(made)
    made = products([moving], behind[:, : 2 * quarter])
    third, handed, made, sums[steps] = phase((third, handed, made, sums[steps]))

    fourth = from_behind(quarters[3], GROUP)
    sums[1] = over_columns(handed)
    handed = to_owners(made)
    made = products([third], behind[:, 2 * quarter : 3 * quarter])
    fourth, sums[1], handed, made = phase((fourth, sums[1], handed, made))

    last = [over_columns(handed)]
    handed = to_owners(made)
    made = products([fourth], behind[:, 3 * quarter :])
    last, handed, made = phase((last, handed, made))

    last.append(over_columns(handed))
    handed = to_owners(made)
    last, handed = phase((last, handed))
    last.append(over_columns(handed))
    sums[0] = jnp.concatenate(last, axis=2)
    stacked = jnp.concatenate(sums)

    def at(offset):
        t = band + place - offset
        return lax.dynamic_index_in_dim(
            stacked, t - t % GROUP + ((t % GROUP) ^ place), 0, keepdims=False
        )

    share = band // n_col
    if n_col == 2:
        band_sum = jnp.stack([at(s + y * share) for s in range(1, share + 1)], axis=1)
        diagonal = lax.dynamic_slice_in_dim(sums[steps][0], y * (block // 2), block // 2, 0)
    else:
        band_sum = jnp.swapaxes(
            lax.psum_scatter(
                jnp.stack([at(s) for s in range(1, band + 1)]),
                "col",
                scatter_dimension=0,
                tiled=True,
            ),
            0,
            1,
        )
        diagonal = lax.psum_scatter(own_products[0], "col", scatter_dimension=0, tiled=True)
    band_new = decay_rate * band_old + (1.0 - decay_rate) * band_sum
    diagonal_new = decay_rate * diagonal_old + (1.0 - decay_rate) * diagonal
    return (band_new, diagonal_new)


def solution(mesh):
    in_specs = (
        P("col", "row"),
        P("row", "col"),
        P("row", "col"),
        P("row", "col", None),
        P(("row", "col"), None),
    )
    out_specs = (P("row", "col", None), P(("row", "col"), None))
    return jax.shard_map(body, mesh=mesh, in_specs=in_specs, out_specs=out_specs, check_vma=False)
```

```python
import jax
import jax.numpy as jnp
from jax import lax
from jax.experimental import pallas as pl
from jax.experimental.pallas import tpu as pltpu
from jax.sharding import PartitionSpec as P

decay_rate = 0.95
GROUP = 4


def swap(array, mask):
    count = lax.axis_size("row")
    return lax.ppermute(array, "row", [(i, i ^ mask) for i in range(count)])


def from_behind(array, by):
    count = lax.axis_size("row")
    return lax.ppermute(array, "row", [(i, (i + by) % count) for i in range(count)])


def trade(array):
    return lax.ppermute(array, "col", [(0, 1), (1, 0)])


def gradient_tile(columns, cotangent_all, accumulated):
    product = lax.dot_general(
        columns, cotangent_all, (((0,), (0,)), ((), ())), preferred_element_type=jnp.float32
    )
    return (product + accumulated.astype(jnp.float32)).astype(jnp.bfloat16)


def block_product(left, right):
    return lax.dot_general(
        left, right, (((1,), (1,)), ((), ())), preferred_element_type=jnp.float32
    )


def products_kernel(*refs):
    *panels, columns, cotangent, out = refs
    lefts, raws = panels[:GROUP], panels[GROUP:]
    raw = jnp.concatenate([piece[...] for piece in raws])
    panel = gradient_tile(columns[...], cotangent[...], raw)
    parts = [block_product(left[...], panel) for left in lefts]

    @pl.when(pl.program_id(0) == 0)
    def _():
        for u, part in enumerate(parts):
            out[u] = part

    @pl.when(pl.program_id(0) > 0)
    def _():
        for u, part in enumerate(parts):
            out[u] += part


def panel_products(group, raws, columns, cotangent_all):
    block, width = group[0].shape
    tokens, rows = columns.shape
    depth = max(d for d in range(128, 1025, 128) if width % d == 0)
    return pl.pallas_call(
        products_kernel,
        grid=(width // depth,),
        in_specs=[pl.BlockSpec((block, depth), lambda k: (0, k))] * len(group)
        + [pl.BlockSpec((raw.shape[0], depth), lambda k: (0, k)) for raw in raws]
        + [
            pl.BlockSpec((tokens, rows), lambda k: (0, 0)),
            pl.BlockSpec((tokens, depth), lambda k: (0, k)),
        ],
        out_specs=pl.BlockSpec((len(group), block, rows), lambda k: (0, 0, 0)),
        out_shape=jax.ShapeDtypeStruct((len(group), block, rows), jnp.float32),
        compiler_params=pltpu.CompilerParams(
            dimension_semantics=("arbitrary",), vmem_limit_bytes=48 * 2**20
        ),
        cost_estimate=pl.CostEstimate(
            flops=2 * rows * width * (len(group) * block + tokens),
            bytes_accessed=2 * width * (len(group) * block + rows + tokens)
            + 4 * len(group) * block * rows,
            transcendentals=0,
        ),
    )(*group, *raws, columns, cotangent_all)


def update_kernel(at_ref, old, *refs):
    out, refs = refs[-1], list(refs[:-1])
    place, y = at_ref[0], at_ref[1]
    own, one = [refs.pop(0) for _ in range(GROUP - 1)], [refs.pop(0) for _ in range(GROUP)]
    two = [(refs[i : i + GROUP], refs[i + GROUP]) for i in range(0, len(refs), GROUP + 1)]
    share = old.shape[1]

    def pick(u, values):
        chosen = values[-1]
        for i in range(len(values) - 1):
            chosen = jnp.where(u == i, values[i], chosen)
        return chosen

    for s in range(share):
        t = 2 * GROUP + place - (s + 1 + y * share)
        u = (t % GROUP) ^ place
        kept, added = decay_rate * old[:, s, :], 1.0 - decay_rate

        @pl.when(t >= 2 * GROUP)
        def _():
            out[:, s, :] = kept + added * pick(u - 1, [ref[...] for ref in own])

        @pl.when((t >= GROUP) & (t < 2 * GROUP))
        def _():
            out[:, s, :] = kept + added * pick(u, [ref[...] for ref in one])

        @pl.when(t < GROUP)
        def _():
            start = 0
            for mine, other in two:
                value = pick(u, [ref[...] for ref in mine]) + other[u].astype(jnp.float32)
                end = start + value.shape[1]
                out[:, s, start:end] = kept[:, start:end] + added * value
                start = end


def update(place, y, band_old, two, one, own):
    block, share, _ = band_old.shape
    rows = block // 4
    operands, specs = [], []
    for piece in [*own, *one]:
        operands.append(piece)
        specs.append(pl.BlockSpec((rows, block), lambda i: (i, 0)))
    for mine, other in two:
        width = other.shape[2]
        operands += [*mine, other]
        specs += [pl.BlockSpec((rows, width), lambda i: (i, 0))] * GROUP
        specs.append(pl.BlockSpec((GROUP, rows, width), lambda i: (0, i, 0)))
    whole = pl.BlockSpec((rows, share, block), lambda i: (i, 0, 0))
    return pl.pallas_call(
        update_kernel,
        grid=(block // rows,),
        in_specs=[pl.BlockSpec(memory_space=pltpu.SMEM), whole, *specs],
        out_specs=whole,
        out_shape=jax.ShapeDtypeStruct(band_old.shape, band_old.dtype),
        compiler_params=pltpu.CompilerParams(
            dimension_semantics=("arbitrary",), vmem_limit_bytes=48 * 2**20
        ),
    )(jnp.stack([place, y]).astype(jnp.int32), band_old, *operands)


def body(activations, cotangent, accumulated, band_old, diagonal_old):
    n_row, n_col = lax.axis_size("row"), lax.axis_size("col")
    block, width = accumulated.shape
    band = n_row // 2
    steps = band // GROUP
    paired = n_col == 2 and steps == 2
    place = lax.axis_index("row") % GROUP
    y = lax.axis_index("col")

    phase = lax.optimization_barrier

    half, quarter = block // 2, block // 4
    moving = [from_behind(accumulated[:half], GROUP), from_behind(accumulated[half:], GROUP)]
    across_raw = swap(accumulated, 2)
    if paired:
        other = trade(activations)
        columns = jnp.where(
            y == 0,
            jnp.concatenate([activations, other]),
            jnp.concatenate([other, activations]),
        )
    else:
        columns = lax.all_gather(activations, "col", axis=0, tiled=True)
    behind = from_behind(columns, GROUP)
    across_columns = swap(columns, 2)
    cotangent_all = lax.all_gather(cotangent, "row", axis=0, tiled=True)

    def products(raws, columns):
        return panel_products(group, raws, columns, cotangent_all)

    def to_owners(made):
        return [made[0]] + [swap(made[u], u) for u in range(1, GROUP)]

    def over_columns(sums):
        if not paired:
            return [None] * len(sums)
        return trade(jnp.stack(sums).astype(jnp.bfloat16))

    def added(sums, others):
        if not paired:
            return sums
        return [a + b.astype(jnp.float32) for a, b in zip(sums, others)]

    own = gradient_tile(columns, cotangent_all, accumulated)
    beside = swap(own, 1)
    moving, behind, own, beside = phase((moving, behind, own, beside))

    sums = [None] * (steps + 1)
    made, diagonal = None, None
    for step in range(1, steps):
        arrived, arrived_columns = moving, behind
        behind = from_behind(arrived_columns, GROUP)
        if step < steps - 1:
            moving = [from_behind(piece, GROUP) for piece in arrived]
        else:
            moving = from_behind(arrived[0], GROUP)
            quarters = jnp.split(arrived[1], 2)
        if step == 1:
            own_products = [block_product(own, panel) for panel in (own, beside)]
            across = gradient_tile(across_columns, cotangent_all, across_raw)
            group = [own, beside, across, swap(across, 1)]
            own_products += [block_product(own, panel) for panel in group[2:]]
            if paired:
                diagonal = lax.dynamic_slice_in_dim(own_products[0], y * half, half, 0) + trade(
                    lax.dynamic_slice_in_dim(own_products[0], (1 - y) * half, half, 0)
                )
                own_products[1:2] = added(own_products[1:2], over_columns(own_products[1:2]))
        else:
            handed = to_owners(made)
            sums[steps - step + 1] = added(handed, over_columns(handed))
        made = products(arrived, arrived_columns)
        if step == steps - 1:
            handed = [made[0], swap(made[1], 1), swap(made[2], 2), made[3]]
            moving, quarters, handed = phase((moving, quarters, handed))
        moving, behind, made, sums, own_products, diagonal = phase(
            (moving, behind, made, sums, own_products, diagonal)
        )

    third = from_behind(quarters[0], GROUP)
    one = added(handed[:3], over_columns(handed[:3]))
    handed = one + [swap(handed[3], 3)]
    made = products([moving], behind[:, :half])
    third, handed, made = phase((third, handed, made))

    fourth = from_behind(quarters[1], GROUP)
    late = [handed[3], *own_products[2:]]
    late = added(late, over_columns(late))
    sums[1] = handed[:3] + late[:1]
    sums[steps] = own_products[:2] + late[1:]
    handed = to_owners(made)
    made = products([third], behind[:, half : half + quarter])
    fourth, sums, handed, made = phase((fourth, sums, handed, made))

    last = [(handed, over_columns(handed))]
    handed = to_owners(made)
    made = products([fourth], behind[:, half + quarter :])
    last, handed, made = phase((last, handed, made))

    last.append((handed, over_columns(handed)))
    handed = to_owners(made)
    last, handed = phase((last, handed))
    last.append((handed, over_columns(handed)))

    if paired:
        band_new = update(place, y, band_old, last, sums[1], sums[2][1:])
    else:
        pieces = [sums_ for sums_, _ in last]
        sums[0] = [jnp.concatenate([piece[u] for piece in pieces], axis=1) for u in range(GROUP)]
        stacked = jnp.stack([piece for row in sums for piece in row])

        def at(offset):
            t = band + place - offset
            return lax.dynamic_index_in_dim(
                stacked, t - t % GROUP + ((t % GROUP) ^ place), 0, keepdims=False
            )

        shares = jnp.stack([at(s) for s in range(1, band + 1)])
        summed = lax.psum_scatter(shares, "col", scatter_dimension=0, tiled=True)
        diagonal = lax.psum_scatter(own_products[0], "col", scatter_dimension=0, tiled=True)
        band_new = decay_rate * band_old + (1.0 - decay_rate) * jnp.swapaxes(summed, 0, 1)
    diagonal_new = decay_rate * diagonal_old + (1.0 - decay_rate) * diagonal
    return (band_new, diagonal_new)


def solution(mesh):
    in_specs = (
        P("col", "row"),
        P("row", "col"),
        P("row", "col"),
        P("row", "col", None),
        P(("row", "col"), None),
    )
    out_specs = (P("row", "col", None), P(("row", "col"), None))
    return jax.shard_map(body, mesh=mesh, in_specs=in_specs, out_specs=out_specs, check_vma=False)
```

```python
import jax
import jax.numpy as jnp
from jax import lax
from jax.experimental import pallas as pl
from jax.experimental.pallas import tpu as pltpu
from jax.sharding import PartitionSpec as P

decay_rate = 0.95
GROUP = 4


def swap(array, mask):
    count = lax.axis_size("row")
    return lax.ppermute(array, "row", [(i, i ^ mask) for i in range(count)])


def from_behind(array, by):
    count = lax.axis_size("row")
    return lax.ppermute(array, "row", [(i, (i + by) % count) for i in range(count)])


def trade(array):
    return lax.ppermute(array, "col", [(0, 1), (1, 0)])


def gradient_tile(columns, cotangent_all, accumulated):
    product = lax.dot_general(
        columns, cotangent_all, (((0,), (0,)), ((), ())), preferred_element_type=jnp.float32
    )
    return (product + accumulated.astype(jnp.float32)).astype(jnp.bfloat16)


def block_product(left, right):
    return lax.dot_general(
        left, right, (((1,), (1,)), ((), ())), preferred_element_type=jnp.float32
    )


def products_kernel(*refs):
    *panels, columns, cotangent, out = refs
    lefts, raws = panels[:GROUP], panels[GROUP:]
    raw = jnp.concatenate([piece[...] for piece in raws])
    panel = gradient_tile(columns[...], cotangent[...], raw)
    parts = [block_product(left[...], panel) for left in lefts]

    @pl.when(pl.program_id(0) == 0)
    def _():
        for u, part in enumerate(parts):
            out[u] = part

    @pl.when(pl.program_id(0) > 0)
    def _():
        for u, part in enumerate(parts):
            out[u] += part


def panel_products(group, raws, columns, cotangent_all):
    block, width = group[0].shape
    tokens, rows = columns.shape
    depth = max(d for d in range(128, 2049, 128) if width % d == 0)
    return pl.pallas_call(
        products_kernel,
        grid=(width // depth,),
        in_specs=[pl.BlockSpec((block, depth), lambda k: (0, k))] * len(group)
        + [pl.BlockSpec((raw.shape[0], depth), lambda k: (0, k)) for raw in raws]
        + [
            pl.BlockSpec((tokens, rows), lambda k: (0, 0)),
            pl.BlockSpec((tokens, depth), lambda k: (0, k)),
        ],
        out_specs=pl.BlockSpec((len(group), block, rows), lambda k: (0, 0, 0)),
        out_shape=jax.ShapeDtypeStruct((len(group), block, rows), jnp.float32),
        compiler_params=pltpu.CompilerParams(
            dimension_semantics=("arbitrary",), vmem_limit_bytes=48 * 2**20
        ),
        cost_estimate=pl.CostEstimate(
            flops=2 * rows * width * (len(group) * block + tokens),
            bytes_accessed=2 * width * (len(group) * block + rows + tokens)
            + 4 * len(group) * block * rows,
            transcendentals=0,
        ),
    )(*group, *raws, columns, cotangent_all)


def update_kernel(at_ref, old, *refs):
    out, refs = refs[-1], list(refs[:-1])
    place, y = at_ref[0], at_ref[1]
    own, one = [refs.pop(0) for _ in range(GROUP - 1)], [refs.pop(0) for _ in range(GROUP)]
    two = [(refs[i : i + GROUP], refs[i + GROUP]) for i in range(0, len(refs), GROUP + 1)]
    share = old.shape[1]

    def pick(u, values):
        chosen = values[-1]
        for i in range(len(values) - 1):
            chosen = jnp.where(u == i, values[i], chosen)
        return chosen

    for s in range(share):
        t = 2 * GROUP + place - (s + 1 + y * share)
        u = (t % GROUP) ^ place
        kept, added = decay_rate * old[:, s, :], 1.0 - decay_rate

        @pl.when(t >= 2 * GROUP)
        def _():
            out[:, s, :] = kept + added * pick(u - 1, [ref[...] for ref in own])

        @pl.when((t >= GROUP) & (t < 2 * GROUP))
        def _():
            out[:, s, :] = kept + added * pick(u, [ref[...] for ref in one])

        @pl.when(t < GROUP)
        def _():
            start = 0
            for mine, other in two:
                value = pick(u, [ref[...].astype(jnp.float32) for ref in mine]) + other[u].astype(jnp.float32)
                end = start + value.shape[1]
                out[:, s, start:end] = kept[:, start:end] + added * value
                start = end


def update(place, y, band_old, two, one, own):
    block, share, _ = band_old.shape
    rows = block // 4
    operands, specs = [], []
    for piece in [*own, *one]:
        operands.append(piece)
        specs.append(pl.BlockSpec((rows, block), lambda i: (i, 0)))
    for mine, other in two:
        width = other.shape[2]
        operands += [*mine, other]
        specs += [pl.BlockSpec((rows, width), lambda i: (i, 0))] * GROUP
        specs.append(pl.BlockSpec((GROUP, rows, width), lambda i: (0, i, 0)))
    whole = pl.BlockSpec((rows, share, block), lambda i: (i, 0, 0))
    return pl.pallas_call(
        update_kernel,
        grid=(block // rows,),
        in_specs=[pl.BlockSpec(memory_space=pltpu.SMEM), whole, *specs],
        out_specs=whole,
        out_shape=jax.ShapeDtypeStruct(band_old.shape, band_old.dtype),
        compiler_params=pltpu.CompilerParams(
            dimension_semantics=("arbitrary",), vmem_limit_bytes=48 * 2**20
        ),
    )(jnp.stack([place, y]).astype(jnp.int32), band_old, *operands)


def body(activations, cotangent, accumulated, band_old, diagonal_old):
    n_row, n_col = lax.axis_size("row"), lax.axis_size("col")
    block, width = accumulated.shape
    band = n_row // 2
    steps = band // GROUP
    paired = n_col == 2 and steps == 2
    place = lax.axis_index("row") % GROUP
    y = lax.axis_index("col")

    phase = lax.optimization_barrier

    half, quarter = block // 2, block // 4
    if paired:
        other = trade(activations)
        columns = jnp.where(
            y == 0,
            jnp.concatenate([activations, other]),
            jnp.concatenate([other, activations]),
        )
    else:
        columns = lax.all_gather(activations, "col", axis=0, tiled=True)
    raw, behind, across_columns = phase(
        (accumulated, from_behind(columns, GROUP), swap(columns, 2))
    )
    moving = from_behind(raw, GROUP)
    across_raw = swap(raw, 2)
    cotangent_all = lax.all_gather(cotangent, "row", axis=0, tiled=True)

    def products(raws, columns):
        return panel_products(group, raws, columns, cotangent_all)

    def to_owners(made):
        return [made[0]] + [swap(made[u], u) for u in range(1, GROUP)]

    def over_columns(sums):
        if not paired:
            return [None] * len(sums)
        return trade(jnp.stack([a.astype(jnp.bfloat16) for a in sums]))

    def added(sums, others):
        if not paired:
            return sums
        return [a + b.astype(jnp.float32) for a, b in zip(sums, others)]

    own = gradient_tile(columns, cotangent_all, accumulated)
    beside = swap(own, 1)
    moving, own, beside = phase((moving, own, beside))

    sums = [None] * (steps + 1)
    made, diagonal = None, None
    for step in range(1, steps):
        arrived, arrived_columns = moving, behind
        behind = from_behind(arrived_columns, GROUP)
        if step < steps - 1:
            moving = from_behind(arrived, GROUP)
        else:
            moving = from_behind(arrived[:half], GROUP)
            quarters = jnp.split(arrived[half:], 2)
        if step == 1:
            own_products = [block_product(own, panel) for panel in (own, beside)]
            across = gradient_tile(across_columns, cotangent_all, across_raw)
            group = [own, beside, across, swap(across, 1)]
            own_products += [block_product(own, panel) for panel in group[2:]]
            if paired:
                diagonal = lax.dynamic_slice_in_dim(own_products[0], y * half, half, 0) + trade(
                    lax.dynamic_slice_in_dim(own_products[0], (1 - y) * half, half, 0)
                )
                own_products[1:2] = added(own_products[1:2], over_columns(own_products[1:2]))
        else:
            handed = to_owners(made)
            sums[steps - step + 1] = added(handed, over_columns(handed))
        made = products([arrived], arrived_columns)
        if step == steps - 1:
            handed = [made[0], swap(made[1], 1), swap(made[2], 2), made[3]]
            moving, quarters, handed = phase((moving, quarters, handed))
        moving, behind, made, sums, own_products, diagonal = phase(
            (moving, behind, made, sums, own_products, diagonal)
        )

    third = from_behind(quarters[0], GROUP)
    one = added(handed[:3], over_columns(handed[:3]))
    handed = one + [swap(handed[3], 3)]
    made = products([moving], behind[:, :half])
    third, handed, made = phase((third, handed, made))

    fourth = from_behind(quarters[1], GROUP)
    late = [handed[3], *own_products[2:]]
    late = added(late, over_columns(late))
    sums[1] = handed[:3] + late[:1]
    sums[steps] = own_products[:2] + late[1:]
    handed = to_owners(made)
    made = products([third], behind[:, half : half + quarter])
    fourth, sums, handed, made = phase((fourth, sums, handed, made))

    last = [(handed, over_columns(handed))]
    handed = to_owners(made)
    made = products([fourth], behind[:, half + quarter :])
    last, handed, made = phase((last, handed, made))

    last.append((handed, over_columns(handed)))
    if paired:
        made = [made[0], *(made[u].astype(jnp.bfloat16) for u in range(1, GROUP))]
    handed = to_owners(made)
    last, handed = phase((last, handed))
    last.append((handed, over_columns(handed)))

    if paired:
        band_new = update(place, y, band_old, last, sums[1], sums[2][1:])
    else:
        pieces = [sums_ for sums_, _ in last]
        sums[0] = [jnp.concatenate([piece[u] for piece in pieces], axis=1) for u in range(GROUP)]
        stacked = jnp.stack([piece for row in sums for piece in row])

        def at(offset):
            t = band + place - offset
            return lax.dynamic_index_in_dim(
                stacked, t - t % GROUP + ((t % GROUP) ^ place), 0, keepdims=False
            )

        shares = jnp.stack([at(s) for s in range(1, band + 1)])
        summed = lax.psum_scatter(shares, "col", scatter_dimension=0, tiled=True)
        diagonal = lax.psum_scatter(own_products[0], "col", scatter_dimension=0, tiled=True)
        band_new = decay_rate * band_old + (1.0 - decay_rate) * jnp.swapaxes(summed, 0, 1)
    diagonal_new = decay_rate * diagonal_old + (1.0 - decay_rate) * diagonal
    return (band_new, diagonal_new)


def solution(mesh):
    in_specs = (
        P("col", "row"),
        P("row", "col"),
        P("row", "col"),
        P("row", "col", None),
        P(("row", "col"), None),
    )
    out_specs = (P("row", "col", None), P(("row", "col"), None))
    return jax.shard_map(body, mesh=mesh, in_specs=in_specs, out_specs=out_specs, check_vma=False)
```

```python
import jax
import jax.numpy as jnp
from jax import lax
from jax.experimental import pallas as pl
from jax.experimental.pallas import tpu as pltpu
from jax.sharding import PartitionSpec as P

decay_rate = 0.95
GROUP = 4


def swap(array, mask):
    count = lax.axis_size("row")
    return lax.ppermute(array, "row", [(i, i ^ mask) for i in range(count)])


def from_behind(array, by):
    count = lax.axis_size("row")
    return lax.ppermute(array, "row", [(i, (i + by) % count) for i in range(count)])


def trade(array):
    return lax.ppermute(array, "col", [(0, 1), (1, 0)])


def gradient_tile(columns, cotangent_all, accumulated):
    product = lax.dot_general(
        columns, cotangent_all, (((0,), (0,)), ((), ())), preferred_element_type=jnp.float32
    )
    return (product + accumulated.astype(jnp.float32)).astype(jnp.bfloat16)


def block_product(left, right):
    return lax.dot_general(
        left, right, (((1,), (1,)), ((), ())), preferred_element_type=jnp.float32
    )


def products_kernel(*refs):
    *panels, columns, cotangent, out = refs
    lefts, raws = panels[:GROUP], panels[GROUP:]
    raw = jnp.concatenate([piece[...] for piece in raws])
    panel = gradient_tile(columns[...], cotangent[...], raw)
    parts = [block_product(left[...], panel) for left in lefts]

    @pl.when(pl.program_id(0) == 0)
    def _():
        for u, part in enumerate(parts):
            out[u] = part

    @pl.when(pl.program_id(0) > 0)
    def _():
        for u, part in enumerate(parts):
            out[u] += part


def panel_products(group, raws, columns, cotangent_all):
    block, width = group[0].shape
    tokens, rows = columns.shape
    depth = max(d for d in range(128, 2049, 128) if width % d == 0)
    return pl.pallas_call(
        products_kernel,
        grid=(width // depth,),
        in_specs=[pl.BlockSpec((block, depth), lambda k: (0, k))] * len(group)
        + [pl.BlockSpec((raw.shape[0], depth), lambda k: (0, k)) for raw in raws]
        + [
            pl.BlockSpec((tokens, rows), lambda k: (0, 0)),
            pl.BlockSpec((tokens, depth), lambda k: (0, k)),
        ],
        out_specs=pl.BlockSpec((len(group), block, rows), lambda k: (0, 0, 0)),
        out_shape=jax.ShapeDtypeStruct((len(group), block, rows), jnp.float32),
        compiler_params=pltpu.CompilerParams(
            dimension_semantics=("arbitrary",), vmem_limit_bytes=48 * 2**20
        ),
        cost_estimate=pl.CostEstimate(
            flops=2 * rows * width * (len(group) * block + tokens),
            bytes_accessed=2 * width * (len(group) * block + rows + tokens)
            + 4 * len(group) * block * rows,
            transcendentals=0,
        ),
    )(*group, *raws, columns, cotangent_all)


def update_kernel(at_ref, old, *refs):
    out, refs = refs[-1], list(refs[:-1])
    place, y = at_ref[0], at_ref[1]
    own, one = [refs.pop(0) for _ in range(GROUP - 1)], [refs.pop(0) for _ in range(GROUP)]
    two = [(refs[i : i + GROUP], refs[i + GROUP]) for i in range(0, len(refs), GROUP + 1)]
    share = old.shape[1]

    def pick(u, values):
        chosen = values[-1]
        for i in range(len(values) - 1):
            chosen = jnp.where(u == i, values[i], chosen)
        return chosen

    for s in range(share):
        t = 2 * GROUP + place - (s + 1 + y * share)
        u = (t % GROUP) ^ place
        kept, added = decay_rate * old[:, s, :], 1.0 - decay_rate

        @pl.when(t >= 2 * GROUP)
        def _():
            out[:, s, :] = kept + added * pick(u - 1, [ref[...] for ref in own])

        @pl.when((t >= GROUP) & (t < 2 * GROUP))
        def _():
            out[:, s, :] = kept + added * pick(u, [ref[...] for ref in one])

        @pl.when(t < GROUP)
        def _():
            start = 0
            for mine, other in two:
                value = pick(u, [ref[...].astype(jnp.float32) for ref in mine]) + other[u].astype(jnp.float32)
                end = start + value.shape[1]
                out[:, s, start:end] = kept[:, start:end] + added * value
                start = end


def update(place, y, band_old, two, one, own):
    block, share, _ = band_old.shape
    rows = block // 4
    operands, specs = [], []
    for piece in [*own, *one]:
        operands.append(piece)
        specs.append(pl.BlockSpec((rows, block), lambda i: (i, 0)))
    for mine, other in two:
        width = other.shape[2]
        operands += [*mine, other]
        specs += [pl.BlockSpec((rows, width), lambda i: (i, 0))] * GROUP
        specs.append(pl.BlockSpec((GROUP, rows, width), lambda i: (0, i, 0)))
    whole = pl.BlockSpec((rows, share, block), lambda i: (i, 0, 0))
    return pl.pallas_call(
        update_kernel,
        grid=(block // rows,),
        in_specs=[pl.BlockSpec(memory_space=pltpu.SMEM), whole, *specs],
        out_specs=whole,
        out_shape=jax.ShapeDtypeStruct(band_old.shape, band_old.dtype),
        compiler_params=pltpu.CompilerParams(
            dimension_semantics=("arbitrary",), vmem_limit_bytes=60 * 2**20
        ),
    )(jnp.stack([place, y]).astype(jnp.int32), band_old, *operands)


def body(activations, cotangent, accumulated, band_old, diagonal_old):
    n_row, n_col = lax.axis_size("row"), lax.axis_size("col")
    block, width = accumulated.shape
    band = n_row // 2
    steps = band // GROUP
    paired = n_col == 2 and steps == 2
    place = lax.axis_index("row") % GROUP
    y = lax.axis_index("col")

    phase = lax.optimization_barrier

    half, quarter = block // 2, block // 4
    raw, *parts = phase(
        (
            accumulated,
            swap(activations, 2),
            *(from_behind(activations, step * GROUP) for step in range(1, steps + 1)),
        )
    )
    moving = from_behind(raw, GROUP)
    across_raw = swap(raw, 2)
    parts = jnp.stack([activations, *parts])
    if paired:
        other = trade(parts)
        parts = jnp.where(
            y == 0,
            jnp.concatenate([parts, other], axis=1),
            jnp.concatenate([other, parts], axis=1),
        )
    else:
        parts = lax.all_gather(parts, "col", axis=1, tiled=True)
    columns, across_columns, *behind = parts
    cotangent_all = lax.all_gather(cotangent, "row", axis=0, tiled=True)

    def products(raws, columns):
        return panel_products(group, raws, columns, cotangent_all)

    def to_owners(made):
        return [made[0]] + [swap(made[u], u) for u in range(1, GROUP)]

    def over_columns(sums):
        if not paired:
            return [None] * len(sums)
        return trade(jnp.stack([a.astype(jnp.bfloat16) for a in sums]))

    def added(sums, others):
        if not paired:
            return sums
        return [a + b.astype(jnp.float32) for a, b in zip(sums, others)]

    own = gradient_tile(columns, cotangent_all, accumulated)
    beside = swap(own, 1)
    moving, own, beside = phase((moving, own, beside))

    sums = [None] * (steps + 1)
    made, diagonal = None, None
    for step in range(1, steps):
        arrived = moving
        if step < steps - 1:
            moving = from_behind(arrived, GROUP)
        else:
            moving = from_behind(arrived[:half], GROUP)
            quarters = jnp.split(arrived[half:], 2)
        if step == 1:
            own_products = [block_product(own, panel) for panel in (own, beside)]
            across = gradient_tile(across_columns, cotangent_all, across_raw)
            group = [own, beside, across, swap(across, 1)]
            own_products += [block_product(own, panel) for panel in group[2:]]
            if paired:
                diagonal = lax.dynamic_slice_in_dim(own_products[0], y * half, half, 0) + trade(
                    lax.dynamic_slice_in_dim(own_products[0], (1 - y) * half, half, 0)
                )
                own_products[1:2] = added(own_products[1:2], over_columns(own_products[1:2]))
        else:
            handed = to_owners(made)
            sums[steps - step + 1] = added(handed, over_columns(handed))
        made = products([arrived], behind[step - 1])
        if step == steps - 1:
            handed = [made[0], swap(made[1], 1), swap(made[2], 2), made[3]]
            moving, quarters, handed = phase((moving, quarters, handed))
        moving, made, sums, own_products, diagonal = phase(
            (moving, made, sums, own_products, diagonal)
        )

    third = from_behind(quarters[0], GROUP)
    one = added(handed[:3], over_columns(handed[:3]))
    handed = one + [swap(handed[3], 3)]
    made = products([moving], behind[-1][:, :half])
    third, handed, made = phase((third, handed, made))

    fourth = from_behind(quarters[1], GROUP)
    late = [handed[3], *own_products[2:]]
    late = added(late, over_columns(late))
    sums[1] = handed[:3] + late[:1]
    sums[steps] = own_products[:2] + late[1:]
    handed = to_owners(made)
    made = products([third], behind[-1][:, half : half + quarter])
    fourth, sums, handed, made = phase((fourth, sums, handed, made))

    last = [(handed, over_columns(handed))]
    handed = to_owners(made)
    made = products([fourth], behind[-1][:, half + quarter :])
    last, handed, made = phase((last, handed, made))

    last.append((handed, over_columns(handed)))
    if paired:
        made = [made[0], *(made[u].astype(jnp.bfloat16) for u in range(1, GROUP))]
    handed = to_owners(made)
    last, handed = phase((last, handed))
    last.append((handed, over_columns(handed)))

    if paired:
        band_new = update(place, y, band_old, last, sums[1], sums[2][1:])
    else:
        pieces = [sums_ for sums_, _ in last]
        sums[0] = [jnp.concatenate([piece[u] for piece in pieces], axis=1) for u in range(GROUP)]
        stacked = jnp.stack([piece for row in sums for piece in row])

        def at(offset):
            t = band + place - offset
            return lax.dynamic_index_in_dim(
                stacked, t - t % GROUP + ((t % GROUP) ^ place), 0, keepdims=False
            )

        shares = jnp.stack([at(s) for s in range(1, band + 1)])
        summed = lax.psum_scatter(shares, "col", scatter_dimension=0, tiled=True)
        diagonal = lax.psum_scatter(own_products[0], "col", scatter_dimension=0, tiled=True)
        band_new = decay_rate * band_old + (1.0 - decay_rate) * jnp.swapaxes(summed, 0, 1)
    diagonal_new = decay_rate * diagonal_old + (1.0 - decay_rate) * diagonal
    return (band_new, diagonal_new)


def solution(mesh):
    in_specs = (
        P("col", "row"),
        P("row", "col"),
        P("row", "col"),
        P("row", "col", None),
        P(("row", "col"), None),
    )
    out_specs = (P("row", "col", None), P(("row", "col"), None))
    return jax.shard_map(body, mesh=mesh, in_specs=in_specs, out_specs=out_specs, check_vma=False)
```

```python
import jax
import jax.numpy as jnp
from jax import lax
from jax.experimental import pallas as pl
from jax.experimental.pallas import tpu as pltpu
from jax.sharding import PartitionSpec as P

decay_rate = 0.95
GROUP = 4


def swap(array, mask):
    count = lax.axis_size("row")
    return lax.ppermute(array, "row", [(i, i ^ mask) for i in range(count)])


def from_behind(array, by):
    count = lax.axis_size("row")
    return lax.ppermute(array, "row", [(i, (i + by) % count) for i in range(count)])


def trade(array):
    return lax.ppermute(array, "col", [(0, 1), (1, 0)])


def gradient_tile(columns, cotangent_all, accumulated):
    product = lax.dot_general(
        columns, cotangent_all, (((0,), (0,)), ((), ())), preferred_element_type=jnp.float32
    )
    return (product + accumulated.astype(jnp.float32)).astype(jnp.bfloat16)


def block_product(left, right):
    return lax.dot_general(
        left, right, (((1,), (1,)), ((), ())), preferred_element_type=jnp.float32
    )


def products_kernel(*refs):
    *panels, columns, cotangent, out = refs
    lefts, raws = panels[:GROUP], panels[GROUP:]
    raw = jnp.concatenate([piece[...] for piece in raws])
    panel = gradient_tile(columns[...], cotangent[...], raw)
    parts = [block_product(left[...], panel) for left in lefts]

    @pl.when(pl.program_id(0) == 0)
    def _():
        for u, part in enumerate(parts):
            out[u] = part

    @pl.when(pl.program_id(0) > 0)
    def _():
        for u, part in enumerate(parts):
            out[u] += part


def panel_products(group, raws, columns, cotangent_all):
    block, width = group[0].shape
    tokens, rows = columns.shape
    depth = max(d for d in range(128, 2049, 128) if width % d == 0)
    return pl.pallas_call(
        products_kernel,
        grid=(width // depth,),
        in_specs=[pl.BlockSpec((block, depth), lambda k: (0, k))] * len(group)
        + [pl.BlockSpec((raw.shape[0], depth), lambda k: (0, k)) for raw in raws]
        + [
            pl.BlockSpec((tokens, rows), lambda k: (0, 0)),
            pl.BlockSpec((tokens, depth), lambda k: (0, k)),
        ],
        out_specs=pl.BlockSpec((len(group), block, rows), lambda k: (0, 0, 0)),
        out_shape=jax.ShapeDtypeStruct((len(group), block, rows), jnp.float32),
        compiler_params=pltpu.CompilerParams(
            dimension_semantics=("arbitrary",), vmem_limit_bytes=48 * 2**20
        ),
        cost_estimate=pl.CostEstimate(
            flops=2 * rows * width * (len(group) * block + tokens),
            bytes_accessed=2 * width * (len(group) * block + rows + tokens)
            + 4 * len(group) * block * rows,
            transcendentals=0,
        ),
    )(*group, *raws, columns, cotangent_all)


def pick(u, values):
    chosen = values[-1]
    for i in range(len(values) - 1):
        chosen = jnp.where(u == i, values[i], chosen)
    return chosen


def update_kernel(at_ref, old, *refs):
    out, refs = refs[-1], list(refs[:-1])
    place, y = at_ref[0], at_ref[1]
    own, one = [refs.pop(0) for _ in range(GROUP - 1)], [refs.pop(0) for _ in range(GROUP)]
    two = [(refs[i : i + GROUP], refs[i + GROUP]) for i in range(0, len(refs), GROUP + 1)]
    share = old.shape[1]
    for s in range(share):
        t = 2 * GROUP + place - (s + 1 + y * share)
        u = (t % GROUP) ^ place
        kept, added = decay_rate * old[:, s, :], 1.0 - decay_rate

        @pl.when(t >= 2 * GROUP)
        def _():
            out[:, s, :] = kept + added * pick(u - 1, [ref[...] for ref in own])

        @pl.when((t >= GROUP) & (t < 2 * GROUP))
        def _():
            out[:, s, :] = kept + added * pick(u, [ref[...] for ref in one])

        @pl.when(t < GROUP)
        def _():
            start = 0
            for mine, other in two:
                value = pick(u, [ref[...].astype(jnp.float32) for ref in mine])
                value += other[u].astype(jnp.float32)
                end = start + value.shape[1]
                out[:, s, start:end] = kept[:, start:end] + added * value
                start = end
            out[:, s, start:] = kept[:, start:]


def last_chunk_kernel(at_ref, band, *refs):
    *mine, other, out = refs
    place, y = at_ref[0], at_ref[1]
    share = band.shape[1]
    for s in range(share):
        t = 2 * GROUP + place - (s + 1 + y * share)
        u = (t % GROUP) ^ place
        value = pick(u, [ref[...].astype(jnp.float32) for ref in mine])
        value += other[u].astype(jnp.float32)
        added = jnp.where(t < GROUP, (1.0 - decay_rate) * value, 0.0)
        out[:, s, :] = band[:, s, :] + added


def update(place, y, band_old, two, one, own):
    block, share, _ = band_old.shape
    rows = block // 4
    at = jnp.stack([place, y]).astype(jnp.int32)
    scalars = pl.BlockSpec(memory_space=pltpu.SMEM)

    def chunk_specs(mine, other):
        width = other.shape[2]
        specs = [pl.BlockSpec((rows, width), lambda i: (i, 0))] * GROUP
        return specs + [pl.BlockSpec((GROUP, rows, width), lambda i: (0, i, 0))]

    params = pltpu.CompilerParams(
        dimension_semantics=("arbitrary",), vmem_limit_bytes=60 * 2**20
    )
    operands, specs = [*own, *one], [pl.BlockSpec((rows, block), lambda i: (i, 0))] * (
        len(own) + len(one)
    )
    for mine, other in two[:-1]:
        operands += [*mine, other]
        specs += chunk_specs(mine, other)
    whole = pl.BlockSpec((rows, share, block), lambda i: (i, 0, 0))
    band = pl.pallas_call(
        update_kernel,
        grid=(block // rows,),
        in_specs=[scalars, whole, *specs],
        out_specs=whole,
        out_shape=jax.ShapeDtypeStruct(band_old.shape, band_old.dtype),
        compiler_params=params,
    )(at, band_old, *operands)
    mine, other = two[-1]
    width = other.shape[2]
    place_of = block // width - 1
    columns = pl.BlockSpec((rows, share, width), lambda i: (i, 0, place_of))
    return pl.pallas_call(
        last_chunk_kernel,
        grid=(block // rows,),
        in_specs=[scalars, columns, *chunk_specs(mine, other)],
        out_specs=columns,
        out_shape=jax.ShapeDtypeStruct(band_old.shape, band_old.dtype),
        input_output_aliases={1: 0},
        compiler_params=params,
    )(at, band, *mine, other)


def body(activations, cotangent, accumulated, band_old, diagonal_old):
    n_row, n_col = lax.axis_size("row"), lax.axis_size("col")
    block, width = accumulated.shape
    band = n_row // 2
    steps = band // GROUP
    paired = n_col == 2 and steps == 2
    place = lax.axis_index("row") % GROUP
    y = lax.axis_index("col")

    phase = lax.optimization_barrier

    half, quarter = block // 2, block // 4
    raw, *parts = phase(
        (
            accumulated,
            swap(activations, 2),
            *(from_behind(activations, step * GROUP) for step in range(1, steps + 1)),
        )
    )
    moving = from_behind(raw, GROUP)
    across_raw = swap(raw, 2)
    parts = jnp.stack([activations, *parts])
    if paired:
        other = trade(parts)
        parts = jnp.where(
            y == 0,
            jnp.concatenate([parts, other], axis=1),
            jnp.concatenate([other, parts], axis=1),
        )
    else:
        parts = lax.all_gather(parts, "col", axis=1, tiled=True)
    columns, across_columns, *behind = parts
    cotangent_all = lax.all_gather(cotangent, "row", axis=0, tiled=True)

    def products(raws, columns):
        return panel_products(group, raws, columns, cotangent_all)

    def to_owners(made):
        return [made[0]] + [swap(made[u], u) for u in range(1, GROUP)]

    def over_columns(sums):
        if not paired:
            return [None] * len(sums)
        return trade(jnp.stack([a.astype(jnp.bfloat16) for a in sums]))

    def added(sums, others):
        if not paired:
            return sums
        return [a + b.astype(jnp.float32) for a, b in zip(sums, others)]

    own = gradient_tile(columns, cotangent_all, accumulated)
    beside = swap(own, 1)
    moving, own, beside = phase((moving, own, beside))

    sums = [None] * (steps + 1)
    made, diagonal = None, None
    for step in range(1, steps):
        arrived = moving
        if step < steps - 1:
            moving = from_behind(arrived, GROUP)
        else:
            moving = from_behind(arrived[:half], GROUP)
            quarters = jnp.split(arrived[half:], 2)
        if step == 1:
            own_products = [block_product(own, panel) for panel in (own, beside)]
            across = gradient_tile(across_columns, cotangent_all, across_raw)
            group = [own, beside, across, swap(across, 1)]
            own_products += [block_product(own, panel) for panel in group[2:]]
            if paired:
                diagonal = lax.dynamic_slice_in_dim(own_products[0], y * half, half, 0) + trade(
                    lax.dynamic_slice_in_dim(own_products[0], (1 - y) * half, half, 0)
                )
                own_products[1:2] = added(own_products[1:2], over_columns(own_products[1:2]))
        else:
            handed = to_owners(made)
            sums[steps - step + 1] = added(handed, over_columns(handed))
        made = products([arrived], behind[step - 1])
        if step == steps - 1:
            handed = [made[0], swap(made[1], 1), swap(made[2], 2), made[3]]
            moving, quarters, handed = phase((moving, quarters, handed))
        moving, made, sums, own_products, diagonal = phase(
            (moving, made, sums, own_products, diagonal)
        )

    third = from_behind(quarters[0], GROUP)
    one = added(handed[:3], over_columns(handed[:3]))
    handed = one + [swap(handed[3], 3)]
    made = products([moving], behind[-1][:, :half])
    third, handed, made = phase((third, handed, made))

    fourth = from_behind(quarters[1], GROUP)
    late = [handed[3], *own_products[2:]]
    late = added(late, over_columns(late))
    sums[1] = handed[:3] + late[:1]
    sums[steps] = own_products[:2] + late[1:]
    handed = to_owners(made)
    made = products([third], behind[-1][:, half : half + quarter])
    fourth, sums, handed, made = phase((fourth, sums, handed, made))

    last = [(handed, over_columns(handed))]
    handed = to_owners(made)
    made = products([fourth], behind[-1][:, half + quarter :])
    last, handed, made = phase((last, handed, made))

    last.append((handed, over_columns(handed)))
    if paired:
        made = [made[0], *(made[u].astype(jnp.bfloat16) for u in range(1, GROUP))]
    handed = to_owners(made)
    last, handed = phase((last, handed))
    last.append((handed, over_columns(handed)))

    if paired:
        band_new = update(place, y, band_old, last, sums[1], sums[2][1:])
    else:
        pieces = [sums_ for sums_, _ in last]
        sums[0] = [jnp.concatenate([piece[u] for piece in pieces], axis=1) for u in range(GROUP)]
        stacked = jnp.stack([piece for row in sums for piece in row])

        def at(offset):
            t = band + place - offset
            return lax.dynamic_index_in_dim(
                stacked, t - t % GROUP + ((t % GROUP) ^ place), 0, keepdims=False
            )

        shares = jnp.stack([at(s) for s in range(1, band + 1)])
        summed = lax.psum_scatter(shares, "col", scatter_dimension=0, tiled=True)
        diagonal = lax.psum_scatter(own_products[0], "col", scatter_dimension=0, tiled=True)
        band_new = decay_rate * band_old + (1.0 - decay_rate) * jnp.swapaxes(summed, 0, 1)
    diagonal_new = decay_rate * diagonal_old + (1.0 - decay_rate) * diagonal
    return (band_new, diagonal_new)


def solution(mesh):
    in_specs = (
        P("col", "row"),
        P("row", "col"),
        P("row", "col"),
        P("row", "col", None),
        P(("row", "col"), None),
    )
    out_specs = (P("row", "col", None), P(("row", "col"), None))
    return jax.shard_map(body, mesh=mesh, in_specs=in_specs, out_specs=out_specs, check_vma=False)
```

```python
import jax
import jax.numpy as jnp
from jax import lax
from jax.experimental import pallas as pl
from jax.experimental.pallas import tpu as pltpu
from jax.sharding import PartitionSpec as P

decay_rate = 0.95
GROUP = 4


def swap(array, mask):
    count = lax.axis_size("row")
    return lax.ppermute(array, "row", [(i, i ^ mask) for i in range(count)])


def from_behind(array, by):
    count = lax.axis_size("row")
    return lax.ppermute(array, "row", [(i, (i + by) % count) for i in range(count)])


def trade(array):
    return lax.ppermute(array, "col", [(0, 1), (1, 0)])


def gradient_tile(columns, cotangent_all, accumulated):
    product = lax.dot_general(
        columns, cotangent_all, (((0,), (0,)), ((), ())), preferred_element_type=jnp.float32
    )
    return (product + accumulated.astype(jnp.float32)).astype(jnp.bfloat16)


def block_product(left, right):
    return lax.dot_general(
        left, right, (((1,), (1,)), ((), ())), preferred_element_type=jnp.float32
    )


def products_kernel(*refs):
    *panels, columns, cotangent, out = refs
    lefts, raws = panels[:GROUP], panels[GROUP:]
    raw = jnp.concatenate([piece[...] for piece in raws])
    panel = gradient_tile(columns[...], cotangent[...], raw)
    parts = [block_product(left[...], panel) for left in lefts]

    @pl.when(pl.program_id(0) == 0)
    def _():
        for u, part in enumerate(parts):
            out[u] = part

    @pl.when(pl.program_id(0) > 0)
    def _():
        for u, part in enumerate(parts):
            out[u] += part


def panel_products(group, raws, columns, cotangent_all):
    block, width = group[0].shape
    tokens, rows = columns.shape
    depth = max(d for d in range(128, 2049, 128) if width % d == 0)
    return pl.pallas_call(
        products_kernel,
        grid=(width // depth,),
        in_specs=[pl.BlockSpec((block, depth), lambda k: (0, k))] * len(group)
        + [pl.BlockSpec((raw.shape[0], depth), lambda k: (0, k)) for raw in raws]
        + [
            pl.BlockSpec((tokens, rows), lambda k: (0, 0)),
            pl.BlockSpec((tokens, depth), lambda k: (0, k)),
        ],
        out_specs=pl.BlockSpec((len(group), block, rows), lambda k: (0, 0, 0)),
        out_shape=jax.ShapeDtypeStruct((len(group), block, rows), jnp.float32),
        compiler_params=pltpu.CompilerParams(
            dimension_semantics=("arbitrary",), vmem_limit_bytes=48 * 2**20
        ),
        cost_estimate=pl.CostEstimate(
            flops=2 * rows * width * (len(group) * block + tokens),
            bytes_accessed=2 * width * (len(group) * block + rows + tokens)
            + 4 * len(group) * block * rows,
            transcendentals=0,
        ),
    )(*group, *raws, columns, cotangent_all)


def pick(u, values):
    chosen = values[-1]
    for i in range(len(values) - 1):
        chosen = jnp.where(u == i, values[i], chosen)
    return chosen


def update_kernel(at_ref, old, *refs):
    out, refs = refs[-1], list(refs[:-1])
    place, y = at_ref[0], at_ref[1]
    own, one = [refs.pop(0) for _ in range(GROUP - 1)], [refs.pop(0) for _ in range(GROUP)]
    two = [(refs[i : i + GROUP], refs[i + GROUP]) for i in range(0, len(refs), GROUP + 1)]
    share = old.shape[1]
    for s in range(share):
        t = 2 * GROUP + place - (s + 1 + y * share)
        u = (t % GROUP) ^ place
        kept, added = decay_rate * old[:, s, :], 1.0 - decay_rate

        @pl.when(t >= 2 * GROUP)
        def _():
            out[:, s, :] = kept + added * pick(u - 1, [ref[...] for ref in own])

        @pl.when((t >= GROUP) & (t < 2 * GROUP))
        def _():
            out[:, s, :] = kept + added * pick(u, [ref[...] for ref in one])

        @pl.when(t < GROUP)
        def _():
            start = 0
            for mine, other in two:
                value = pick(u, [ref[...].astype(jnp.float32) for ref in mine])
                value += other[u].astype(jnp.float32)
                end = start + value.shape[1]
                out[:, s, start:end] = kept[:, start:end] + added * value
                start = end
            out[:, s, start:] = kept[:, start:]


def last_chunk_kernel(at_ref, band, *refs):
    *mine, other, out = refs
    place, y = at_ref[0], at_ref[1]
    share = band.shape[1]
    for s in range(share):
        t = 2 * GROUP + place - (s + 1 + y * share)
        u = (t % GROUP) ^ place
        value = pick(u, [ref[...].astype(jnp.float32) for ref in mine])
        value += other[u].astype(jnp.float32)
        added = jnp.where(t < GROUP, (1.0 - decay_rate) * value, 0.0)
        out[:, s, :] = band[:, s, :] + added


def update(place, y, band_old, two, one, own):
    block, share, _ = band_old.shape
    rows = block // 4
    at = jnp.stack([place, y]).astype(jnp.int32)
    scalars = pl.BlockSpec(memory_space=pltpu.SMEM)

    def chunk_specs(mine, other):
        width = other.shape[2]
        specs = [pl.BlockSpec((rows, width), lambda i: (i, 0))] * GROUP
        return specs + [pl.BlockSpec((GROUP, rows, width), lambda i: (0, i, 0))]

    params = pltpu.CompilerParams(
        dimension_semantics=("arbitrary",), vmem_limit_bytes=60 * 2**20
    )
    operands, specs = [*own, *one], [pl.BlockSpec((rows, block), lambda i: (i, 0))] * (
        len(own) + len(one)
    )
    for mine, other in two[:-1]:
        operands += [*mine, other]
        specs += chunk_specs(mine, other)
    whole = pl.BlockSpec((rows, share, block), lambda i: (i, 0, 0))
    band = pl.pallas_call(
        update_kernel,
        grid=(block // rows,),
        in_specs=[scalars, whole, *specs],
        out_specs=whole,
        out_shape=jax.ShapeDtypeStruct(band_old.shape, band_old.dtype),
        compiler_params=params,
    )(at, band_old, *operands)
    mine, other = two[-1]
    width = other.shape[2]
    place_of = block // width - 1
    columns = pl.BlockSpec((rows, share, width), lambda i: (i, 0, place_of))
    return pl.pallas_call(
        last_chunk_kernel,
        grid=(block // rows,),
        in_specs=[scalars, columns, *chunk_specs(mine, other)],
        out_specs=columns,
        out_shape=jax.ShapeDtypeStruct(band_old.shape, band_old.dtype),
        input_output_aliases={1: 0},
        compiler_params=params,
    )(at, band, *mine, other)


def body(activations, cotangent, accumulated, band_old, diagonal_old):
    n_row, n_col = lax.axis_size("row"), lax.axis_size("col")
    block, width = accumulated.shape
    band = n_row // 2
    steps = band // GROUP
    paired = n_col == 2 and steps == 2
    place = lax.axis_index("row") % GROUP
    y = lax.axis_index("col")

    phase = lax.optimization_barrier

    half, quarter = block // 2, block // 4
    raw, *parts = phase(
        (
            accumulated,
            swap(activations, 2),
            *(from_behind(activations, step * GROUP) for step in range(1, steps + 1)),
        )
    )
    moving = from_behind(raw, GROUP)
    across_raw = swap(raw, 2)
    parts = jnp.stack([activations, *parts])
    if paired:
        other = trade(parts)
        parts = jnp.where(
            y == 0,
            jnp.concatenate([parts, other], axis=1),
            jnp.concatenate([other, parts], axis=1),
        )
    else:
        parts = lax.all_gather(parts, "col", axis=1, tiled=True)
    columns, across_columns, *behind = parts
    cotangent_all = lax.all_gather(cotangent, "row", axis=0, tiled=True)

    def products(raws, columns):
        return panel_products(group, raws, columns, cotangent_all)

    def to_owners(made):
        return [made[0]] + [swap(made[u], u) for u in range(1, GROUP)]

    def over_columns(sums):
        if not paired:
            return [None] * len(sums)
        return trade(jnp.stack([a.astype(jnp.bfloat16) for a in sums]))

    def added(sums, others):
        if not paired:
            return sums
        return [a + b.astype(jnp.float32) for a, b in zip(sums, others)]

    own = gradient_tile(columns, cotangent_all, accumulated)
    beside = swap(own, 1)
    moving, own, beside = phase((moving, own, beside))

    sums = [None] * (steps + 1)
    made, diagonal = None, None
    for step in range(1, steps):
        arrived = moving
        if step < steps - 1:
            moving = from_behind(arrived, GROUP)
        else:
            moving = from_behind(arrived[:half], GROUP)
            quarters = jnp.split(arrived[half:], 2)
        if step == 1:
            own_products = [block_product(own, panel) for panel in (own, beside)]
            across = gradient_tile(across_columns, cotangent_all, across_raw)
            group = [own, beside, across, swap(across, 1)]
            own_products += [block_product(own, panel) for panel in group[2:]]
            if paired:
                diagonal = lax.dynamic_slice_in_dim(own_products[0], y * half, half, 0) + trade(
                    lax.dynamic_slice_in_dim(own_products[0], (1 - y) * half, half, 0)
                )
                own_products[1:2] = added(own_products[1:2], over_columns(own_products[1:2]))
        else:
            handed = to_owners(made)
            sums[steps - step + 1] = added(handed, over_columns(handed))
        made = products([arrived], behind[step - 1])
        if step == steps - 1:
            handed = [made[0], swap(made[1], 1), swap(made[2], 2), made[3]]
            moving, quarters, handed = phase((moving, quarters, handed))
        moving, made, sums, own_products, diagonal = phase(
            (moving, made, sums, own_products, diagonal)
        )

    third = from_behind(quarters[0], GROUP)
    one = added(handed[:3], over_columns(handed[:3]))
    handed = one + [swap(handed[3], 3)]
    made = products([moving], behind[-1][:, :half])
    third, handed, made = phase((third, handed, made))

    fourth = from_behind(quarters[1], GROUP)
    late = [handed[3], *own_products[2:]]
    late = added(late, over_columns(late))
    sums[1] = handed[:3] + late[:1]
    sums[steps] = own_products[:2] + late[1:]
    handed = to_owners(made)
    made = products([third], behind[-1][:, half : half + quarter])
    fourth, sums, handed, made = phase((fourth, sums, handed, made))

    last = [(handed, over_columns(handed))]
    handed = to_owners(made)
    made = products([fourth], behind[-1][:, half + quarter :])
    handed, made = phase((handed, made))

    last.append((handed, over_columns(handed)))
    if paired:
        made = [made[0], *(made[u].astype(jnp.bfloat16) for u in range(1, GROUP))]
    handed = to_owners(made)
    handed = phase(handed)
    last.append((handed, over_columns(handed)))

    if paired:
        band_new = update(place, y, band_old, last, sums[1], sums[2][1:])
    else:
        pieces = [sums_ for sums_, _ in last]
        sums[0] = [jnp.concatenate([piece[u] for piece in pieces], axis=1) for u in range(GROUP)]
        stacked = jnp.stack([piece for row in sums for piece in row])

        def at(offset):
            t = band + place - offset
            return lax.dynamic_index_in_dim(
                stacked, t - t % GROUP + ((t % GROUP) ^ place), 0, keepdims=False
            )

        shares = jnp.stack([at(s) for s in range(1, band + 1)])
        summed = lax.psum_scatter(shares, "col", scatter_dimension=0, tiled=True)
        diagonal = lax.psum_scatter(own_products[0], "col", scatter_dimension=0, tiled=True)
        band_new = decay_rate * band_old + (1.0 - decay_rate) * jnp.swapaxes(summed, 0, 1)
    diagonal_new = decay_rate * diagonal_old + (1.0 - decay_rate) * diagonal
    return (band_new, diagonal_new)


def solution(mesh):
    in_specs = (
        P("col", "row"),
        P("row", "col"),
        P("row", "col"),
        P("row", "col", None),
        P(("row", "col"), None),
    )
    out_specs = (P("row", "col", None), P(("row", "col"), None))
    return jax.shard_map(body, mesh=mesh, in_specs=in_specs, out_specs=out_specs, check_vma=False)
```
